128 devices in a mesh: dp: 8 (over x_hi, y), fsdp: 16 (over x_lo, z, core).
Axes of the slice: x: 4 (x_hi: 2, x_lo: 2; x = x_hi * 2 + x_lo), y: 4, z: 4, core: 2. Of those that a mesh axis runs over, the one named last changes fastest.
Arguments:
- queries: bfloat16 [16384, 2048], P(('dp', 'fsdp')), may hold values from -16 to 16
- doc_kv: bfloat16 [2, 8, 512, 2048], P(None, 'dp', 'fsdp'), may hold values from -12 to 12
- residual: bfloat16 [16384, 4096], P(('dp', 'fsdp')), may hold values from -25 to 25
- out_weight: bfloat16 [2048, 4096], P(None, 'fsdp'), may hold values from -0.125 to 0.125
- out_gain: float32 [4096], replicated, may hold values from 0.1 to 1.9
- head: bfloat16 [16384, 4096], P('fsdp')
- source: int32 [8], replicated, may hold values from 0 to 7, each once
- lengths: int32 [8, 8], P('dp'), may hold values from 1 to 256, 1280 in all within a row
- sampled: int32 [16384], P(('dp', 'fsdp')), may hold values from 0 to 16383
- old_logprob: float32 [16384], P(('dp', 'fsdp')), may hold values from -13 to -7
Outputs:
- log_ratio: float32 [16384], P(('dp', 'fsdp'))
- kl_term: float32 [16384], P(('dp', 'fsdp'))
The draws below stay inside these ranges and needn't reach their ends.
Inputs may be any that keep to these rules, and one draw needn't show every extreme that they name: Each row of lengths sums to 1280. `source`: each document appears once.
All inputs are finite; a program needn't handle non-finite values.
Results may differ from the reference program's by a relative error of at most 0.0028.
Values may be sent and summed in bfloat16 or wider, within the bound.
A program may use at most 128 MiB of HBM per device.

```python
import math
import jax
import jax.numpy as jnp
import numpy as np
from jax import lax

D = 4096
HEAD_DIM = 256
HEADS = 8
VOCAB = 16384
DOC_LEN = 512
SUM_LEN = 256
SUMS = 8
TOKENS = 16384
N_DP = 8


def draw_queries(key, part):
    key = jax.random.fold_in(key, 1)
    noise = 2.0 * jnp.clip(jax.random.normal(key, (TOKENS, HEADS * HEAD_DIM), jnp.float32), -3.0, 3.0)
    return noise.astype(jnp.bfloat16)


def draw_doc_kv(key, part):
    width = HEADS * HEAD_DIM
    key = jax.random.fold_in(key, 2)
    keys = jnp.clip(jax.random.normal(jax.random.fold_in(key, 3), (N_DP, DOC_LEN, width), jnp.float32), -4.0, 4.0)
    values = 3.0 * jnp.clip(jax.random.normal(jax.random.fold_in(key, 4), (N_DP, DOC_LEN, width), jnp.float32), -4.0, 4.0)
    return jnp.stack([keys, values]).astype(jnp.bfloat16)


def draw_residual(key, part):
    key = jax.random.fold_in(key, 5)
    base = jnp.clip(jax.random.normal(key, (TOKENS, D), jnp.float32), -5.0, 5.0)
    return base.astype(jnp.bfloat16)


def draw_head(key, part):
    key = jax.random.fold_in(key, 6)
    base = jnp.clip(jax.random.normal(key, (VOCAB, D), jnp.float32), -3.0, 3.0) * float(D) ** (-0.5)
    return base.astype(jnp.bfloat16)


def place_ends(array, rng, smallest, high):
    longest = array.shape.index(max(array.shape))
    spots = []
    for shift in (0, 1):
        where = [jax.random.randint(jax.random.fold_in(rng, axis), (), 0, length) for axis, length in enumerate(array.shape)]
        where[longest] = (where[longest] + shift) % array.shape[longest]
        spots.append(tuple(where))
    return array.at[spots[0]].set(smallest).at[spots[1]].set(high)


def block_levels(own_key, extent, split, low, high):
    gain = 1.0
    for dim, blocks in split:
        heights = jax.random.uniform(jax.random.fold_in(jax.random.fold_in(own_key, 6), dim), (blocks,), jnp.float32, low / len(split), high / len(split))
        gain = gain * jnp.repeat(jnp.exp(heights), extent[dim] // blocks).reshape((-1,) + (1,) * (len(extent) - 1 - dim))
    return gain


def profile(number_of, total, most, lean):
    loads = [(1 << 20) // math.isqrt(rank ** lean) + 1 for rank in range(2, number_of + 1)]
    surplus, counts = total - most - (number_of - 1), [1] * (number_of - 1)
    while surplus > 0:
        free = [i for i in range(number_of - 1) if counts[i] < most]
        mass, left = sum([loads[i] for i in free]), surplus
        for i in free:
            more = min(most - counts[i], max(1, left * loads[i] // mass), surplus)
            counts[i] = counts[i] + more
            surplus = surplus - more
    return np.array([most] + counts)


def uneven_parts(own_key, count, total, most, slope):
    if count == 2:
        one = jax.random.randint(own_key, (), max(1, total - most), min(most, total - 1) + 1)
        return jnp.stack([one, total - one])
    tallies = jnp.asarray(profile(count, total, most, slope), jnp.int32)
    twos = (count - 1) // 2
    donor, taker = tallies[1:1 + 2 * twos:2], tallies[2:2 + 2 * twos:2]
    margin = jnp.minimum(donor - 1, most - taker)
    passed = jax.random.randint(jax.random.fold_in(own_key, 1), (twos,), 0, 1 << 20) % (margin + 1)
    tallies = tallies.at[1:1 + 2 * twos:2].set(donor - passed).at[2:2 + 2 * twos:2].set(taker + passed)
    return tallies[jax.random.permutation(jax.random.fold_in(own_key, 2), count)]


def normal_values(stream_key, dims, deviation, most, shards=(), kind=jnp.bfloat16):
    gain = block_levels(stream_key, dims, shards, -0.22, 0.18) if shards else 1.0
    values = jax.random.normal(stream_key, dims, jnp.float32) * deviation * gain
    return jnp.minimum(jnp.maximum(values, -most), most).astype(kind)


def setup_inputs(seed: int = 0) -> dict:
    streams_of = jax.random.split(jax.random.key(seed), 11)
    return {
        "queries": draw_queries(jax.random.fold_in(streams_of[10], 71), 0),
        "doc_kv": draw_doc_kv(jax.random.fold_in(streams_of[10], 71), 0),
        "residual": draw_residual(jax.random.fold_in(streams_of[10], 71), 0),
        "out_weight": normal_values(streams_of[3], (HEADS * HEAD_DIM, D), (HEADS * HEAD_DIM) ** -0.5, 0.125, ((1, 16),)),
        "out_gain": jnp.clip(1.0 + 0.18 * jax.random.normal(streams_of[4], (D,), jnp.float32), 0.1, 1.9),
        "head": draw_head(jax.random.fold_in(streams_of[10], 71), 0),
        "source": jax.random.permutation(streams_of[6], N_DP).astype(jnp.int32),
        "lengths": jax.vmap(lambda own: uneven_parts(own, SUMS, SUMS * SUM_LEN * 5 // 8, SUM_LEN, 1))(jax.random.split(streams_of[7], N_DP)).reshape((N_DP, SUMS)).astype(jnp.int32),
        "sampled": place_ends(jax.random.randint(streams_of[8], (TOKENS,), 0, VOCAB), jax.random.fold_in(streams_of[8], 1), 0, VOCAB - 1).astype(jnp.int32),
        "old_logprob": jnp.clip(-13.0 + 6.0 * jax.random.uniform(streams_of[9], (TOKENS,), jnp.float32) ** block_levels(streams_of[9], (TOKENS,), ((0, 128),), -0.2, 0.2), -13.0, -7.0),
    }


def attend(query_rows, keys, values):
    count = query_rows.shape[0]
    width = query_rows.shape[1]
    q3 = query_rows.reshape(count, HEADS, HEAD_DIM).astype(jnp.float32)
    k3 = keys.reshape(keys.shape[0], HEADS, HEAD_DIM).astype(jnp.float32)
    v3 = values.reshape(values.shape[0], HEADS, HEAD_DIM).astype(jnp.float32)
    scores = jnp.einsum('thd,lhd->htl', q3, k3) * float(HEAD_DIM) ** (-0.5)
    largest = lax.optimization_barrier(jnp.max(scores, axis=2, keepdims=True))
    raised = jnp.exp(scores - largest)
    weights = (raised / lax.optimization_barrier(jnp.sum(raised, axis=2, keepdims=True))).astype(jnp.bfloat16)
    mixed = jnp.einsum('htl,lhd->thd', weights.astype(jnp.float32), v3)
    return mixed.reshape(count, width).astype(jnp.bfloat16)

def reference(queries, doc_kv, residual, out_weight, out_gain, head, source, lengths, sampled, old_logprob):
    row_slots = SUMS * SUM_LEN

    def one_row(index):
        chosen = source[index]
        keys = lax.dynamic_index_in_dim(doc_kv[0], chosen, 0, keepdims=False)
        values = lax.dynamic_index_in_dim(doc_kv[1], chosen, 0, keepdims=False)
        first = (index * row_slots).astype(jnp.int32)
        query_rows = lax.dynamic_slice_in_dim(queries, first, row_slots, 0)
        base_rows = lax.dynamic_slice_in_dim(residual, first, row_slots, 0)
        token_ids = lax.dynamic_slice_in_dim(sampled, first, row_slots, 0)
        attended = attend(query_rows, keys, values)
        summed = jnp.dot(attended, out_weight, preferred_element_type=jnp.float32) + base_rows.astype(jnp.float32)
        scale = lax.rsqrt(lax.optimization_barrier(jnp.mean(summed * summed, axis=1, keepdims=True)) + 1e-06)
        hidden = (summed * scale * out_gain[None, :]).astype(jnp.bfloat16)
        logits = jnp.dot(hidden, head.T, preferred_element_type=jnp.float32)
        largest = lax.optimization_barrier(jnp.max(logits, axis=1))
        total = lax.optimization_barrier(jnp.sum(jnp.exp(logits - largest[:, None]), axis=1))
        picked = jnp.take_along_axis(logits, token_ids[:, None], axis=1)[:, 0]
        return picked - (largest + jnp.log(total))
    new_logprob = lax.map(one_row, jnp.arange(N_DP, dtype=jnp.int32)).reshape(TOKENS)
    slots = jnp.arange(TOKENS, dtype=jnp.int32)
    position = slots % SUM_LEN
    summary = slots // SUM_LEN
    limit = lengths.reshape(-1)[summary]
    live = position < limit
    log_ratio = jnp.where(live, new_logprob - old_logprob, jnp.float32(0.0))
    gap = jnp.clip(old_logprob - new_logprob, -3.0, 3.0)
    kl_term = jnp.where(live, jnp.exp(gap) - gap - 1.0, jnp.float32(0.0))
    return (log_ratio, kl_term)
```

```python
import jax
import jax.numpy as jnp
from jax import lax
from jax.experimental import pallas as pl
from jax.experimental.pallas import tpu as pltpu
from jax.sharding import PartitionSpec as P

HEADS = 8
DEPTH = 256
GROUP = 16
ROWS = 8
MESH = pl.DeviceIdType.MESH
PIECES = 4


class Gather:
    def __init__(self, me, buf, own, send_sem, recv_sem, pieces):
        self.me, self.buf, self.own = me, buf, own
        self.send_sem, self.recv_sem = send_sem, recv_sem
        self.pieces = pieces
        self.rows = buf.shape[2] // pieces
        x, z, core = me // 8, (me // 2) % 4, me % 2

        def slot(dx, dz):
            return ((x + dx) % 2) * 8 + ((z + dz) % 4) * 2 + core

        self.x, self.zp, self.zm, self.z2 = slot(1, 0), slot(0, 1), slot(0, 3), slot(0, 2)
        self.xzp, self.xzm, self.xz2 = slot(1, 1), slot(1, 3), slot(1, 2)
        self.core = me + 1 - 2 * core

    def at(self, ref, slot, half, p):
        return ref.at[slot, half, pl.ds(p * self.rows, self.rows)]

    def send(self, slot, half, p, *targets, own=False):
        dst = self.at(self.buf, slot, half, p)
        src = self.own.at[half, pl.ds(p * self.rows, self.rows)] if own else dst
        for target in targets:
            pltpu.make_async_remote_copy(
                src_ref=src,
                dst_ref=dst,
                send_sem=self.send_sem,
                recv_sem=self.recv_sem.at[slot, half, p],
                device_id={"fsdp": target},
                device_id_type=MESH,
            ).start()

    def wait(self, slot, half, p):
        view = self.at(self.buf, slot, half, p)
        pltpu.make_async_copy(view, view, self.recv_sem.at[slot, half, p]).wait()

    def each(self, step):
        if self.pieces == 1:
            step(0)
        else:
            pl.loop(0, self.pieces)(step)

    def wave1(self):
        def first(p):
            self.send(self.me, 0, p, self.x, own=True)
            self.send(self.me, 1, p, self.zp, self.zm, own=True)

        def second(p):
            self.send(self.me, 1, p, self.x, self.core, own=True)
            self.send(self.me, 0, p, self.zp, self.zm, self.core, own=True)

        self.each(first)
        self.each(second)

    def wave2(self):
        def step(p):
            self.wait(self.x, 0, p)
            self.send(self.x, 0, p, self.zp, self.zm, self.core)
            self.wait(self.zp, 1, p)
            self.send(self.zp, 1, p, self.zm, self.x, self.core)
            self.wait(self.zm, 1, p)
            self.send(self.zm, 1, p, self.x, self.core)

        self.each(step)

    def wave3(self):
        def step(p):
            self.wait(self.zm, 0, p)
            self.send(self.zm, 0, p, self.zp, self.core)
            self.wait(self.zp, 0, p)
            self.send(self.zp, 0, p, self.core)
            self.wait(self.x, 1, p)
            self.send(self.x, 1, p, self.core)

        def later(p):
            self.wait(self.z2, 1, p)
            self.send(self.z2, 1, p, self.x, self.core)
            self.wait(self.xzm, 0, p)
            self.send(self.xzm, 0, p, self.zp, self.core)
            self.wait(self.xzp, 0, p)
            self.send(self.xzp, 0, p, self.core)

        self.each(step)
        self.each(later)

    def wave4(self):
        def step(p):
            for slot, half in ((self.xzp, 1), (self.xzm, 1), (self.z2, 0)):
                self.wait(slot, half, p)
                self.send(slot, half, p, self.core)

        def later(p):
            for slot, half in ((self.xz2, 0), (self.xz2, 1)):
                self.wait(slot, half, p)
                self.send(slot, half, p, self.core)

        self.each(step)
        self.each(later)

    def wait_slot(self, slot):
        for half in range(2):
            self.each(lambda p: self.wait(slot, half, p))

    def wait_siblings(self):
        other = self.core % 2

        @pl.loop(0, GROUP // 2)
        def _(k):
            self.wait_slot(2 * k + other)

    def drain(self):
        view = self.buf.at[pl.ds(0, 15)]
        pltpu.make_async_copy(view, view, self.send_sem).wait()


def kernel(
    source,
    lengths,
    ids,
    old,
    gain,
    q_hbm,
    doc_hbm,
    res_hbm,
    w_hbm,
    head_hbm,
    ratio_out,
    kl_out,
    head,
    wbuf,
    hbuf,
    dbuf,
    kv,
    q,
    res,
    att,
    summed,
    logits,
    idbuf,
    stat_out,
    stat_in,
    local_sems,
    w_send,
    w_recv,
    h_send,
    h_recv,
    kv_send,
    kv_recv,
    dp_send,
    dp_recv,
    id_send,
    id_recv,
    stat_send,
    stat_recv,
):
    row = lax.axis_index("dp")
    me = lax.axis_index("fsdp")

    barrier = pltpu.get_barrier_semaphore()

    @pl.loop(1, GROUP)
    def _(j):
        pl.semaphore_signal(barrier, inc=1, device_id={"fsdp": (me + j) % GROUP}, device_id_type=MESH)

    @pl.loop(1, ROWS)
    def _(j):
        pl.semaphore_signal(barrier, inc=1, device_id={"dp": (row + j) % ROWS}, device_id_type=MESH)

    locals_ = [
        pltpu.make_async_copy(doc_hbm, dbuf.at[row], local_sems.at[0]),
        pltpu.make_async_copy(q_hbm, q, local_sems.at[1]),
        pltpu.make_async_copy(res_hbm, res, local_sems.at[2]),
        pltpu.make_async_copy(w_hbm, wbuf.at[me], local_sems.at[3]),
        pltpu.make_async_copy(head_hbm, head, local_sems.at[4]),
    ]
    for copy in locals_:
        copy.start()
    idbuf[me] = jnp.broadcast_to(ids[...], (8, 128))

    pl.semaphore_wait(barrier, GROUP + ROWS - 2)

    @pl.loop(1, ROWS)
    def _(j):
        pltpu.make_async_remote_copy(
            src_ref=doc_hbm,
            dst_ref=dbuf.at[row],
            send_sem=dp_send,
            recv_sem=dp_recv.at[row],
            device_id={"dp": (row + j) % ROWS},
            device_id_type=MESH,
        ).start()

    wg = Gather(me, wbuf, w_hbm, w_send, w_recv, PIECES)
    hg = Gather(me, hbuf, hbuf.at[me], h_send, h_recv, PIECES)
    dg = Gather(me, kv, kv.at[me], kv_send, kv_recv, 1)
    wg.wave1()

    @pl.loop(1, GROUP)
    def _(j):
        pltpu.make_async_remote_copy(
            src_ref=idbuf.at[me],
            dst_ref=idbuf.at[me],
            send_sem=id_send,
            recv_sem=id_recv.at[me],
            device_id={"fsdp": (me + j) % GROUP},
            device_id_type=MESH,
        ).start()

    wg.wave2()

    @pl.loop(1, ROWS)
    def _(j):
        other = (row + j) % ROWS
        pltpu.make_async_copy(dbuf.at[other], dbuf.at[other], dp_recv.at[other]).wait()

    locals_[0].wait()
    kv[me] = dbuf[source[row]]
    dg.wave1()
    wg.wave3()
    dg.wave2()
    dg.wave3()
    wg.wave4()
    dg.wave4()
    dg.wait_siblings()

    locals_[1].wait()

    @pl.loop(0, HEADS)
    def _(h):
        columns = pl.ds(pl.multiple_of(h * DEPTH, DEPTH), DEPTH)
        keys = kv[:, 0, :, columns].reshape(-1, DEPTH)
        values = kv[:, 1, :, columns].reshape(-1, DEPTH)
        scores = lax.dot_general(
            q[:, columns], keys, (((1,), (1,)), ((), ())), preferred_element_type=jnp.float32
        ) * float(DEPTH) ** (-0.5)
        raised = jnp.exp(scores - jnp.max(scores, axis=1, keepdims=True))
        weights = (raised / jnp.sum(raised, axis=1, keepdims=True)).astype(jnp.bfloat16)
        att[:, columns] = jnp.dot(weights, values, preferred_element_type=jnp.float32).astype(jnp.bfloat16)

    locals_[2].wait()
    locals_[3].wait()
    wg.wait_siblings()

    width = wbuf.shape[3]

    def project(k, squares):
        columns = pl.ds(pl.multiple_of(k * width, width), width)
        part = jnp.dot(
            att[...], wbuf[k].reshape(-1, width), preferred_element_type=jnp.float32
        ) + res[:, columns].astype(jnp.float32)
        summed[:, columns] = part
        return squares + part * part

    squares = lax.fori_loop(0, GROUP, project, jnp.zeros((128, width), jnp.float32))
    mean = jnp.sum(squares, axis=1, keepdims=True) / summed.shape[1]
    scale = lax.rsqrt(mean + 1e-06)

    @pl.loop(0, GROUP)
    def _(k):
        columns = pl.ds(pl.multiple_of(k * width, width), width)
        hidden = (summed[:, columns] * scale * gain[:, columns]).astype(jnp.bfloat16)
        hbuf[me, :, :, columns] = hidden.reshape(2, 64, width)

    hg.wave1()
    locals_[4].wait()

    @pl.loop(1, GROUP)
    def _(j):
        other = (me + j) % GROUP
        pltpu.make_async_copy(idbuf.at[other], idbuf.at[other], id_recv.at[other]).wait()

    first_id = me * head.shape[0]
    vocab = lax.broadcasted_iota(jnp.int32, (head.shape[0], 128), 0) + first_id

    @pl.loop(0, 8)
    def _(step):
        @pl.when(step == 1)
        def _():
            hg.wave2()
            hg.wave3()

        @pl.when(step == 4)
        def _():
            hg.wave4()

        dx = jnp.where((step == 1) | (step > 4), 1, 0)
        turn = jnp.where(step > 4, step - 4, jnp.where(step > 1, step - 1, 0))
        dz = jnp.where(turn == 2, 3, jnp.where(turn == 3, 2, turn))
        chip = ((me // 8 + dx) % 2) * 4 + ((me // 2) % 4 + dz) % 4
        hg.wait_slot(2 * chip + hg.core % 2)
        tokens = hbuf[pl.ds(2 * chip, 2)].reshape(256, -1)
        logits[...] = lax.dot_general(
            head[...], tokens, (((1,), (1,)), ((), ())), preferred_element_type=jnp.float32
        )
        for c in range(2):
            slot = 2 * chip + c
            block = logits[:, c * 128 : (c + 1) * 128]
            largest = jnp.max(block, axis=0, keepdims=True)
            total = jnp.sum(jnp.exp(block - largest), axis=0, keepdims=True)
            picked = jnp.sum(jnp.where(vocab == idbuf[slot][0:1], block, 0.0), axis=0, keepdims=True)
            stat_out[slot, 0:1] = largest
            stat_out[slot, 1:2] = total
            stat_out[slot, 2:3] = picked
            stat_out[slot, 3:8] = jnp.zeros((5, 128), jnp.float32)

    @pl.loop(1, GROUP)
    def _(j):
        other = (me + j) % GROUP
        pltpu.make_async_remote_copy(
            src_ref=stat_out.at[other],
            dst_ref=stat_in.at[me],
            send_sem=stat_send,
            recv_sem=stat_recv.at[me],
            device_id={"fsdp": other},
            device_id_type=MESH,
        ).start()

    stat_in[me] = stat_out[me]

    @pl.loop(1, GROUP)
    def _(j):
        other = (me + j) % GROUP
        pltpu.make_async_copy(stat_in.at[other], stat_in.at[other], stat_recv.at[other]).wait()

    largest = stat_in[:, 0, :]
    highest = jnp.max(largest, axis=0, keepdims=True)
    total = jnp.sum(stat_in[:, 1, :] * jnp.exp(largest - highest), axis=0, keepdims=True)
    picked = jnp.sum(stat_in[:, 2, :], axis=0, keepdims=True)
    new = picked - (highest + jnp.log(total))
    position = (me % 2) * 128 + lax.broadcasted_iota(jnp.int32, (1, 128), 1)
    live = position < lengths[0, me // 2]
    before = old[...]
    ratio_out[...] = jnp.where(live, new - before, 0.0)
    gap = jnp.clip(before - new, -3.0, 3.0)
    kl_out[...] = jnp.where(live, jnp.exp(gap) - gap - 1.0, 0.0)

    wg.drain()
    hg.drain()
    dg.drain()
    for buf, count, sem in ((dbuf, 7, dp_send), (idbuf, 15, id_send), (stat_out, 15, stat_send)):
        view = buf.at[pl.ds(0, count)]
        pltpu.make_async_copy(view, view, sem).wait()


def on_device(
    queries, doc_kv, residual, out_weight, out_gain, head, source, lengths, sampled, old_logprob
):
    tokens, width = queries.shape
    columns = residual.shape[1]
    share = out_weight.shape[1]
    bf16, f32 = jnp.bfloat16, jnp.float32
    smem = pl.BlockSpec(memory_space=pltpu.SMEM)
    vmem = pl.BlockSpec(memory_space=pltpu.VMEM)
    any_ = pl.BlockSpec(memory_space=pl.ANY)
    dma = pltpu.SemaphoreType.DMA
    out = jax.ShapeDtypeStruct((1, tokens), f32)
    ratio, kl = pl.pallas_call(
        kernel,
        out_shape=(out, out),
        in_specs=[smem, smem, vmem, vmem, vmem] + [any_] * 5,
        out_specs=(vmem, vmem),
        scratch_shapes=[
            pltpu.VMEM(head.shape, bf16),
            pltpu.VMEM((GROUP, 2, width // 2, share), bf16),
            pltpu.VMEM((GROUP, 2, tokens // 2, columns), bf16),
            pltpu.VMEM((ROWS, 2, doc_kv.shape[2], width), bf16),
            pltpu.VMEM((GROUP, 2, doc_kv.shape[2], width), bf16),
            pltpu.VMEM((tokens, width), bf16),
            pltpu.VMEM((tokens, columns), bf16),
            pltpu.VMEM((tokens, width), bf16),
            pltpu.VMEM((tokens, columns), f32),
            pltpu.VMEM((head.shape[0], 256), f32),
            pltpu.VMEM((GROUP, 8, 128), jnp.int32),
            pltpu.VMEM((GROUP, 8, 128), f32),
            pltpu.VMEM((GROUP, 8, 128), f32),
            dma((5,)),
            dma,
            dma((GROUP, 2, PIECES)),
            dma,
            dma((GROUP, 2, PIECES)),
            dma,
            dma((GROUP, 2, 1)),
            dma,
            dma((ROWS,)),
            dma,
            dma((GROUP,)),
            dma,
            dma((GROUP,)),
        ],
        compiler_params=pltpu.CompilerParams(
            collective_id=0, has_side_effects=True, vmem_limit_bytes=60 * 1024 * 1024
        ),
    )(
        source,
        lengths,
        sampled.reshape(1, tokens),
        old_logprob.reshape(1, tokens),
        out_gain.reshape(1, columns),
        queries,
        doc_kv.reshape(2, doc_kv.shape[2], width),
        residual,
        out_weight.reshape(2, width // 2, share),
        head,
    )
    return ratio.reshape(tokens), kl.reshape(tokens)


def solution(mesh):
    return jax.shard_map(
        on_device,
        mesh=mesh,
        in_specs=(
            P(("dp", "fsdp"), None),
            P(None, "dp", "fsdp", None),
            P(("dp", "fsdp"), None),
            P(None, "fsdp"),
            P(),
            P("fsdp", None),
            P(),
            P("dp", None),
            P(("dp", "fsdp")),
            P(("dp", "fsdp")),
        ),
        out_specs=(P(("dp", "fsdp")), P(("dp", "fsdp"))),
        check_vma=False,
    )
```

```python
import jax
import jax.numpy as jnp
from jax import lax
from jax.experimental import pallas as pl
from jax.experimental.pallas import tpu as pltpu
from jax.sharding import PartitionSpec as P

HEADS = 8
DEPTH = 256
GROUP = 16
ROWS = 8
MESH = pl.DeviceIdType.MESH
PIECES = 4


class Gather:
    def __init__(self, me, buf, own, send_sem, recv_sem, pieces):
        self.me, self.buf, self.own = me, buf, own
        self.send_sem, self.recv_sem = send_sem, recv_sem
        self.pieces = pieces
        self.rows = buf.shape[2] // pieces
        x, z, core = me // 8, (me // 2) % 4, me % 2

        def slot(dx, dz):
            return ((x + dx) % 2) * 8 + ((z + dz) % 4) * 2 + core

        self.x, self.zp, self.zm, self.z2 = slot(1, 0), slot(0, 1), slot(0, 3), slot(0, 2)
        self.xzp, self.xzm, self.xz2 = slot(1, 1), slot(1, 3), slot(1, 2)
        self.core = me + 1 - 2 * core

    def at(self, ref, slot, half, p):
        return ref.at[slot, half, pl.ds(p * self.rows, self.rows)]

    def send(self, slot, half, p, *targets, own=False):
        dst = self.at(self.buf, slot, half, p)
        src = self.own.at[half, pl.ds(p * self.rows, self.rows)] if own else dst
        for target in targets:
            pltpu.make_async_remote_copy(
                src_ref=src,
                dst_ref=dst,
                send_sem=self.send_sem,
                recv_sem=self.recv_sem.at[slot, half, p],
                device_id={"fsdp": target},
                device_id_type=MESH,
            ).start()

    def wait(self, slot, half, p):
        view = self.at(self.buf, slot, half, p)
        pltpu.make_async_copy(view, view, self.recv_sem.at[slot, half, p]).wait()

    def each(self, step):
        if self.pieces == 1:
            step(0)
        else:
            pl.loop(0, self.pieces)(step)

    def wave1(self):
        def first(p):
            self.send(self.me, 0, p, self.x, own=True)
            self.send(self.me, 1, p, self.zp, self.zm, own=True)

        def second(p):
            self.send(self.me, 1, p, self.x, self.core, own=True)
            self.send(self.me, 0, p, self.zp, self.zm, self.core, own=True)

        self.each(first)
        self.each(second)

    def wave2(self):
        def step(p):
            self.wait(self.x, 0, p)
            self.send(self.x, 0, p, self.zp, self.zm, self.core)
            self.wait(self.zp, 1, p)
            self.send(self.zp, 1, p, self.zm, self.x, self.core)
            self.wait(self.zm, 1, p)
            self.send(self.zm, 1, p, self.x, self.core)

        self.each(step)

    def wave3(self):
        def step(p):
            self.wait(self.zm, 0, p)
            self.send(self.zm, 0, p, self.zp, self.core)
            self.wait(self.zp, 0, p)
            self.send(self.zp, 0, p, self.core)
            self.wait(self.x, 1, p)
            self.send(self.x, 1, p, self.core)

        def later(p):
            self.wait(self.z2, 1, p)
            self.send(self.z2, 1, p, self.x, self.core)
            self.wait(self.xzm, 0, p)
            self.send(self.xzm, 0, p, self.zp, self.core)
            self.wait(self.xzp, 0, p)
            self.send(self.xzp, 0, p, self.core)

        self.each(step)
        self.each(later)

    def wave4a(self):
        def step(p):
            for slot, half in ((self.xzp, 1), (self.xzm, 1)):
                self.wait(slot, half, p)
                self.send(slot, half, p, self.core)

        self.each(step)

    def wave4b(self):
        def step(p):
            for slot, half in ((self.z2, 0), (self.xz2, 0), (self.xz2, 1)):
                self.wait(slot, half, p)
                self.send(slot, half, p, self.core)

        self.each(step)

    def wait_slot(self, slot):
        for half in range(2):
            self.each(lambda p: self.wait(slot, half, p))

    def wait_siblings(self):
        other = self.core % 2

        @pl.loop(0, GROUP // 2)
        def _(k):
            self.wait_slot(2 * k + other)

    def drain(self):
        view = self.buf.at[pl.ds(0, 15)]
        pltpu.make_async_copy(view, view, self.send_sem).wait()


def kernel(
    source,
    lengths,
    ids,
    old,
    gain,
    q_hbm,
    doc_hbm,
    res_hbm,
    w_hbm,
    head_hbm,
    ratio_out,
    kl_out,
    head,
    wbuf,
    hbuf,
    dbuf,
    kv,
    qbuf,
    rbuf,
    att,
    summed,
    logits,
    idbuf,
    sq_out,
    sq_in,
    stat_out,
    stat_in,
    local_sems,
    head_sem,
    w_send,
    w_recv,
    h_send,
    h_recv,
    kv_send,
    kv_recv,
    dp_send,
    dp_recv,
    q_send,
    q_recv,
    r_send,
    r_recv,
    att_send,
    att_recv,
    sq_send,
    sq_recv,
    id_send,
    id_recv,
    stat_send,
    stat_recv,
):
    row = lax.axis_index("dp")
    me = lax.axis_index("fsdp")
    x, z, core = me // 8, (me // 2) % 4, me % 2
    xh, y = row // 4, row % 4
    quad = x * 2 + core
    share = wbuf.shape[3]
    tokens = qbuf.shape[1]

    def device(dx, dz, dc):
        return ((x + dx) % 2) * 8 + ((z + dz) % 4) * 2 + (core + dc) % 2

    def doc_row(dh, dy):
        return ((xh + dh) % 2) * 4 + (y + dy) % 4

    def columns_of(other, k):
        block = (other // 8) * 8 + k * 2 + other % 2
        return pl.ds(pl.multiple_of(block * share, share), share)

    def remote(src, dst, send, recv, **where):
        pltpu.make_async_remote_copy(
            src_ref=src, dst_ref=dst, send_sem=send, recv_sem=recv, device_id=where, device_id_type=MESH
        ).start()

    def arrived(view, sem):
        pltpu.make_async_copy(view, view, sem).wait()

    barrier = pltpu.get_barrier_semaphore()

    @pl.loop(1, GROUP)
    def _(j):
        pl.semaphore_signal(barrier, inc=1, device_id={"fsdp": (me + j) % GROUP}, device_id_type=MESH)

    near_rows = (doc_row(1, 0), doc_row(0, 1), doc_row(0, 3))
    for other in near_rows:
        pl.semaphore_signal(barrier, inc=1, device_id={"dp": other}, device_id_type=MESH)

    locals_ = [
        pltpu.make_async_copy(doc_hbm, dbuf.at[row], local_sems.at[0]),
        pltpu.make_async_copy(q_hbm, qbuf.at[x], local_sems.at[1]),
        pltpu.make_async_copy(w_hbm, wbuf.at[z], local_sems.at[2]),
    ] + [
        pltpu.make_async_copy(
            res_hbm.at[:, columns_of(me, k)],
            rbuf.at[quad, :, pl.ds(k * share, share)],
            local_sems.at[3 + k],
        )
        for k in range(4)
    ]
    for copy in locals_:
        copy.start()
    for k in range(GROUP):
        pltpu.make_async_copy(
            head_hbm.at[:, pl.ds(k * share, share)],
            head.at[(k // 8) * 2 + k % 2, :, pl.ds((k // 2) % 4 * share, share)],
            head_sem,
        ).start()
    idbuf[me] = jnp.broadcast_to(ids[...], (8, 128))

    pl.semaphore_wait(barrier, GROUP - 1 + 3)

    def send_doc(slot, halves, *targets, own=False):
        for half in halves:
            for target in targets:
                dst = dbuf.at[slot, half]
                remote(doc_hbm.at[half] if own else dst, dst, dp_send, dp_recv.at[slot, half], dp=target)

    def wait_doc(slot, half):
        arrived(dbuf.at[slot, half], dp_recv.at[slot, half])

    send_doc(row, (0, 1), *near_rows, own=True)
    remote(q_hbm, qbuf.at[x], q_send, q_recv, fsdp=device(1, 0, 0))

    w_rows = wbuf.shape[2] // PIECES

    def w_at(slot, half, p):
        return wbuf.at[slot, half, pl.ds(p * w_rows, w_rows)]

    def send_w(slot, half, p, *targets, own=False):
        dst = w_at(slot, half, p)
        src = w_hbm.at[half, pl.ds(p * w_rows, w_rows)] if own else dst
        for target in targets:
            remote(src, dst, w_send, w_recv.at[slot, half, p], fsdp=target)

    def wait_w(slot, half, p):
        arrived(w_at(slot, half, p), w_recv.at[slot, half, p])

    zp, zm = (z + 1) % 4, (z + 3) % 4

    @pl.loop(0, PIECES)
    def _(p):
        send_w(z, 0, p, device(0, 1, 0), own=True)
        send_w(z, 1, p, device(0, 3, 0), own=True)

    @pl.loop(0, PIECES)
    def _(p):
        send_w(z, 1, p, device(0, 1, 0), own=True)
        send_w(z, 0, p, device(0, 3, 0), own=True)

    partner, up, down = doc_row(1, 0), doc_row(0, 1), doc_row(0, 3)
    for half in range(2):
        wait_doc(partner, half)
        send_doc(partner, (half,), up, down)

    quad_peers = (device(1, 0, 0), device(0, 0, 1), device(1, 0, 1))
    for other in quad_peers:
        for k in range(4):
            remote(
                res_hbm.at[:, columns_of(other, k)],
                rbuf.at[quad, :, pl.ds(k * share, share)],
                r_send,
                r_recv.at[quad],
                fsdp=other,
            )

    @pl.loop(1, GROUP)
    def _(j):
        remote(idbuf.at[me], idbuf.at[me], id_send, id_recv.at[me], fsdp=(me + j) % GROUP)

    for dh in range(2):
        wait_doc(doc_row(dh, 3), 0)
        send_doc(doc_row(dh, 3), (0,), up)
        wait_doc(doc_row(dh, 1), 1)
        send_doc(doc_row(dh, 1), (1,), down)

    @pl.loop(0, PIECES)
    def _(p):
        wait_w(zm, 0, p)
        send_w(zm, 0, p, device(0, 1, 0))
        wait_w(zp, 1, p)
        send_w(zp, 1, p, device(0, 3, 0))

    for dh in range(2):
        wait_doc(doc_row(dh, 3), 1)
        wait_doc(doc_row(dh, 1), 0)
        for half in range(2):
            wait_doc(doc_row(dh, 2), half)
    locals_[0].wait()

    hg = Gather(me, hbuf, hbuf.at[me], h_send, h_recv, PIECES)
    dg = Gather(me, kv, kv.at[me], kv_send, kv_recv, 1)
    kv[me] = dbuf[source[row]]
    dg.wave1()
    dg.wave2()
    dg.wave3()
    dg.wave4a()
    dg.wave4b()
    dg.wait_siblings()

    locals_[1].wait()
    arrived(qbuf.at[1 - x], q_recv)

    @pl.loop(0, HEADS)
    def _(h):
        columns = pl.ds(pl.multiple_of(h * DEPTH, DEPTH), DEPTH)
        keys = kv[:, 0, :, columns].reshape(-1, DEPTH)
        values = kv[:, 1, :, columns].reshape(-1, DEPTH)
        scores = lax.dot_general(
            qbuf[:, :, columns].reshape(-1, DEPTH),
            keys,
            (((1,), (1,)), ((), ())),
            preferred_element_type=jnp.float32,
        ) * float(DEPTH) ** (-0.5)
        raised = jnp.exp(scores - jnp.max(scores, axis=1, keepdims=True))
        weights = (raised / jnp.sum(raised, axis=1, keepdims=True)).astype(jnp.bfloat16)
        mixed = jnp.dot(weights, values, preferred_element_type=jnp.float32).astype(jnp.bfloat16)
        att[core, :, :, columns] = mixed.reshape(2, tokens, DEPTH)

    remote(att.at[core], att.at[core], att_send, att_recv, fsdp=device(0, 0, 1))

    for copy in locals_[2:]:
        copy.wait()

    @pl.loop(0, PIECES)
    def _(p):
        wait_w(zp, 0, p)
        wait_w(zm, 1, p)
        wait_w((z + 2) % 4, 0, p)
        wait_w((z + 2) % 4, 1, p)

    for other in quad_peers:
        slot = (other // 8) * 2 + other % 2
        arrived(rbuf.at[slot], r_recv.at[slot])
    arrived(att.at[1 - core], att_recv)

    def project(k, squares):
        columns = pl.ds(pl.multiple_of(k * share, share), share)
        weight = wbuf[k].reshape(-1, share)
        both = [
            jnp.dot(att[c].reshape(2 * tokens, -1), weight, preferred_element_type=jnp.float32)
            for c in range(2)
        ]
        out = []
        for slot in range(4):
            mixed = both[slot % 2][(slot // 2) * tokens : (slot // 2 + 1) * tokens]
            part = mixed + rbuf[slot, :, columns].astype(jnp.float32)
            summed[slot, :, columns] = part
            out.append(squares[slot] + part * part)
        return tuple(out)

    zero = jnp.zeros((tokens, share), jnp.float32)
    squares = lax.fori_loop(0, 4, project, (zero,) * 4)
    for slot in range(4):
        own = jnp.sum(squares[slot], axis=1, keepdims=True)
        sq_out[slot] = jnp.broadcast_to(own, (tokens, 128)).T[0:8]
    for other in quad_peers:
        remote(sq_out, sq_in.at[quad], sq_send, sq_recv.at[quad], fsdp=other)
    sq_in[quad] = sq_out[...]
    for other in quad_peers:
        slot = (other // 8) * 2 + other % 2
        arrived(sq_in.at[slot], sq_recv.at[slot])
    mean = (sq_in[0] + sq_in[1] + sq_in[2] + sq_in[3]) / head_hbm.shape[1]
    scale = lax.rsqrt(mean + 1e-06)
    for slot in range(4):
        factor = jnp.broadcast_to(scale[slot, 0:1], (128, tokens)).T[:, 0:1]
        for k in range(4):
            columns = pl.ds(k * share, share)
            hidden = summed[slot, :, columns] * factor * gain[:, columns_of(me, k)]
            hbuf[me, slot // 2, pl.ds((slot % 2) * tokens, tokens), columns] = hidden.astype(jnp.bfloat16)

    hg.wave1()
    arrived(head, head_sem)

    @pl.loop(1, GROUP)
    def _(j):
        other = (me + j) % GROUP
        arrived(idbuf.at[other], id_recv.at[other])

    vocab = lax.broadcasted_iota(jnp.int32, (head.shape[1], 128), 0) + me * head.shape[1]

    @pl.loop(0, 8)
    def _(step):
        @pl.when(step == 0)
        def _():
            hg.wave2()

        @pl.when(step == 1)
        def _():
            hg.wave3()

        @pl.when(step == 4)
        def _():
            hg.wave4a()

        @pl.when(step == 6)
        def _():
            hg.wave4b()

        middle = (step >= 2) & (step < 6)
        half = jnp.where(middle, (step - 2) // 2, step % 2)
        dz = jnp.where(step < 2, 0, jnp.where(step >= 6, 2, 1 + 2 * (step % 2)))
        spot = (z + dz) % 4
        for dx in range(2):
            slot = dx * 8 + spot * 2 + 1 - core
            hg.each(lambda p: hg.wait(slot, half, p))
        total = None
        for k in range(4):
            slot = (k // 2) * 8 + spot * 2 + k % 2
            part = lax.dot_general(
                head[k], hbuf[slot, half], (((1,), (1,)), ((), ())), preferred_element_type=jnp.float32
            )
            total = part if total is None else total + part
        logits[...] = total
        for c in range(2):
            slot = half * 8 + spot * 2 + c
            block = logits[:, c * 128 : (c + 1) * 128]
            largest = jnp.max(block, axis=0, keepdims=True)
            total = jnp.sum(jnp.exp(block - largest), axis=0, keepdims=True)
            picked = jnp.sum(jnp.where(vocab == idbuf[slot][0:1], block, 0.0), axis=0, keepdims=True)
            stat_out[slot, 0:1] = largest
            stat_out[slot, 1:2] = total
            stat_out[slot, 2:3] = picked
            stat_out[slot, 3:8] = jnp.zeros((5, 128), jnp.float32)

    @pl.loop(1, GROUP)
    def _(j):
        other = (me + j) % GROUP
        remote(stat_out.at[other], stat_in.at[me], stat_send, stat_recv.at[me], fsdp=other)

    stat_in[me] = stat_out[me]

    @pl.loop(1, GROUP)
    def _(j):
        other = (me + j) % GROUP
        arrived(stat_in.at[other], stat_recv.at[other])

    largest = stat_in[:, 0, :]
    highest = jnp.max(largest, axis=0, keepdims=True)
    total = jnp.sum(stat_in[:, 1, :] * jnp.exp(largest - highest), axis=0, keepdims=True)
    picked = jnp.sum(stat_in[:, 2, :], axis=0, keepdims=True)
    new = picked - (highest + jnp.log(total))
    position = core * tokens + lax.broadcasted_iota(jnp.int32, (1, 128), 1)
    live = position < lengths[0, me // 2]
    before = old[...]
    ratio_out[...] = jnp.where(live, new - before, 0.0)
    gap = jnp.clip(before - new, -3.0, 3.0)
    kl_out[...] = jnp.where(live, jnp.exp(gap) - gap - 1.0, 0.0)

    hg.drain()
    dg.drain()
    for buf, count, sem in (
        (wbuf, 3, w_send),
        (dbuf, 7, dp_send),
        (rbuf, 3, r_send),
        (qbuf, 1, q_send),
        (att, 1, att_send),
        (sq_in, 3, sq_send),
        (idbuf, 15, id_send),
        (stat_out, 15, stat_send),
    ):
        view = buf.at[pl.ds(0, count)]
        arrived(view, sem)


def on_device(
    queries, doc_kv, residual, out_weight, out_gain, head, source, lengths, sampled, old_logprob
):
    tokens, width = queries.shape
    columns = residual.shape[1]
    share = out_weight.shape[1]
    positions = doc_kv.shape[2]
    bf16, f32 = jnp.bfloat16, jnp.float32
    smem = pl.BlockSpec(memory_space=pltpu.SMEM)
    vmem = pl.BlockSpec(memory_space=pltpu.VMEM)
    any_ = pl.BlockSpec(memory_space=pl.ANY)
    dma = pltpu.SemaphoreType.DMA
    out = jax.ShapeDtypeStruct((1, tokens), f32)
    ratio, kl = pl.pallas_call(
        kernel,
        out_shape=(out, out),
        in_specs=[smem, smem, vmem, vmem, vmem] + [any_] * 5,
        out_specs=(vmem, vmem),
        scratch_shapes=[
            pltpu.VMEM((4, head.shape[0], columns // 4), bf16),
            pltpu.VMEM((4, 2, width // 2, share), bf16),
            pltpu.VMEM((GROUP, 2, 2 * tokens, columns // 4), bf16),
            pltpu.VMEM((ROWS, 2, positions, width), bf16),
            pltpu.VMEM((GROUP, 2, positions, width), bf16),
            pltpu.VMEM((2, tokens, width), bf16),
            pltpu.VMEM((4, tokens, columns // 4), bf16),
            pltpu.VMEM((2, 2, tokens, width), bf16),
            pltpu.VMEM((4, tokens, columns // 4), f32),
            pltpu.VMEM((head.shape[0], 256), f32),
            pltpu.VMEM((GROUP, 8, 128), jnp.int32),
            pltpu.VMEM((4, 8, 128), f32),
            pltpu.VMEM((4, 4, 8, 128), f32),
            pltpu.VMEM((GROUP, 8, 128), f32),
            pltpu.VMEM((GROUP, 8, 128), f32),
            dma((7,)),
            dma,
            dma,
            dma((4, 2, PIECES)),
            dma,
            dma((GROUP, 2, PIECES)),
            dma,
            dma((GROUP, 2, 1)),
            dma,
            dma((ROWS, 2)),
            dma,
            dma,
            dma,
            dma((4,)),
            dma,
            dma,
            dma,
            dma((4,)),
            dma,
            dma((GROUP,)),
            dma,
            dma((GROUP,)),
        ],
        compiler_params=pltpu.CompilerParams(
            collective_id=0, has_side_effects=True, vmem_limit_bytes=60 * 1024 * 1024
        ),
    )(
        source,
        lengths,
        sampled.reshape(1, tokens),
        old_logprob.reshape(1, tokens),
        out_gain.reshape(1, columns),
        queries,
        doc_kv.reshape(2, positions, width),
        residual,
        out_weight.reshape(2, width // 2, share),
        head,
    )
    return ratio.reshape(tokens), kl.reshape(tokens)


def solution(mesh):
    return jax.shard_map(
        on_device,
        mesh=mesh,
        in_specs=(
            P(("dp", "fsdp"), None),
            P(None, "dp", "fsdp", None),
            P(("dp", "fsdp"), None),
            P(None, "fsdp"),
            P(),
            P("fsdp", None),
            P(),
            P("dp", None),
            P(("dp", "fsdp")),
            P(("dp", "fsdp")),
        ),
        out_specs=(P(("dp", "fsdp")), P(("dp", "fsdp"))),
        check_vma=False,
    )
```

```python
import jax
import jax.numpy as jnp
from jax import lax
from jax.experimental import pallas as pl
from jax.experimental.pallas import tpu as pltpu
from jax.sharding import PartitionSpec as P

HEADS = 8
DEPTH = 256
GROUP = 16
ROWS = 8
MESH = pl.DeviceIdType.MESH
PIECES = 4
HIDDEN = 16
VIA_X = 9


class Gather:
    def __init__(self, me, view, own, send_sem, recv_sem, first, second):
        self.me, self.view, self.own = me, view, own
        self.send_sem, self.recv_sem = send_sem, recv_sem
        self.first, self.second = first, second
        self.middle = (second[0] + second[1] + 1) // 2
        x, z, core = me // 8, (me // 2) % 4, me % 2

        def slot(dx, dz):
            return ((x + dx) % 2) * 8 + ((z + dz) % 4) * 2 + core

        self.x, self.zp, self.zm, self.z2 = slot(1, 0), slot(0, 1), slot(0, 3), slot(0, 2)
        self.xzp, self.xzm, self.xz2 = slot(1, 1), slot(1, 3), slot(1, 2)
        self.core = me + 1 - 2 * core

    def send(self, slot, p, *targets, own=False):
        dst = self.view(slot, p)
        src = self.own(p) if own else dst
        for target in targets:
            pltpu.make_async_remote_copy(
                src_ref=src,
                dst_ref=dst,
                send_sem=self.send_sem,
                recv_sem=self.recv_sem.at[slot, p],
                device_id={"fsdp": target},
                device_id_type=MESH,
            ).start()

    def wait(self, slot, p):
        view = self.view(slot, p)
        pltpu.make_async_copy(view, view, self.recv_sem.at[slot, p]).wait()

    def pass_on(self, slot, p, *targets):
        self.wait(slot, p)
        self.send(slot, p, *targets, self.core)

    def each(self, low, high, step):
        if high - low == 1:
            step(low)
        elif high > low:
            pl.loop(low, high)(step)

    def wave1(self):
        self.each(*self.first, lambda p: self.send(self.me, p, self.x, own=True))
        self.each(*self.second, lambda p: self.send(self.me, p, self.zp, self.zm, own=True))
        self.each(*self.first, lambda p: self.send(self.me, p, self.zp, self.zm, self.core, own=True))
        self.each(*self.second, lambda p: self.send(self.me, p, self.x, self.core, own=True))

    def wave2(self):
        self.each(*self.first, lambda p: self.pass_on(self.x, p, self.zp, self.zm))

    def wave3(self):
        def up(p):
            self.pass_on(self.zp, p, self.x)
            self.pass_on(self.zm, p, self.zp, self.x)

        def down(p):
            self.pass_on(self.zp, p, self.zm, self.x)
            self.pass_on(self.zm, p, self.x)

        def own_side(p):
            self.pass_on(self.zm, p, self.zp)
            self.pass_on(self.zp, p)

        self.each(self.middle, self.second[1], up)
        self.each(self.second[0], self.middle, down)
        self.each(*self.first, own_side)
        self.each(*self.second, lambda p: self.pass_on(self.x, p))

    def wave4(self):
        def far_side(p):
            self.pass_on(self.xzp, p, self.zm)
            self.pass_on(self.xzm, p)

        self.each(*self.first, far_side)

    def wave5(self):
        def far_side(p):
            self.pass_on(self.xzp, p)
            self.pass_on(self.xzm, p)

        self.each(*self.second, lambda p: self.pass_on(self.z2, p, self.x))
        self.each(*self.second, far_side)

    def last(self, low, high):
        def step(p):
            self.pass_on(self.z2, p)
            self.pass_on(self.xz2, p)

        self.each(max(low, self.first[0]), min(high, self.first[1]), step)
        self.each(
            max(low, self.second[0]), min(high, self.second[1]), lambda p: self.pass_on(self.xz2, p)
        )


def kernel(
    source,
    lengths,
    ids,
    old,
    gain,
    q_hbm,
    doc_hbm,
    res_hbm,
    w_hbm,
    head_hbm,
    ratio_out,
    kl_out,
    head,
    wbuf,
    hbuf,
    dbuf,
    kv,
    qbuf,
    rbuf,
    att,
    summed,
    logits,
    idbuf,
    sq_out,
    sq_in,
    stat_out,
    stat_in,
    local_sems,
    head_sem,
    w_send,
    w_recv,
    h_send,
    h_recv,
    kv_send,
    kv_recv,
    dp_send,
    dp_recv,
    q_send,
    q_recv,
    r_send,
    r_recv,
    att_send,
    att_recv,
    sq_send,
    sq_recv,
    id_send,
    id_recv,
    stat_send,
    stat_recv,
):
    row = lax.axis_index("dp")
    me = lax.axis_index("fsdp")
    x, z, core = me // 8, (me // 2) % 4, me % 2
    xh, y = row // 4, row % 4
    quad = x * 2 + core
    share = wbuf.shape[3]
    tokens = qbuf.shape[1]

    def device(dx, dz, dc):
        return ((x + dx) % 2) * 8 + ((z + dz) % 4) * 2 + (core + dc) % 2

    def doc_row(dh, dy):
        return ((xh + dh) % 2) * 4 + (y + dy) % 4

    def columns_of(other, k):
        block = (other // 8) * 8 + k * 2 + other % 2
        return pl.ds(pl.multiple_of(block * share, share), share)

    def remote(src, dst, send, recv, **where):
        pltpu.make_async_remote_copy(
            src_ref=src, dst_ref=dst, send_sem=send, recv_sem=recv, device_id=where, device_id_type=MESH
        ).start()

    def arrived(view, sem):
        pltpu.make_async_copy(view, view, sem).wait()

    barrier = pltpu.get_barrier_semaphore()

    @pl.loop(1, GROUP)
    def _(j):
        pl.semaphore_signal(barrier, inc=1, device_id={"fsdp": (me + j) % GROUP}, device_id_type=MESH)

    near_rows = (doc_row(1, 0), doc_row(0, 1), doc_row(0, 3))
    for other in near_rows:
        pl.semaphore_signal(barrier, inc=1, device_id={"dp": other}, device_id_type=MESH)

    locals_ = [
        pltpu.make_async_copy(doc_hbm, dbuf.at[row], local_sems.at[0]),
        pltpu.make_async_copy(q_hbm, qbuf.at[x], local_sems.at[1]),
        pltpu.make_async_copy(w_hbm, wbuf.at[z], local_sems.at[2]),
    ] + [
        pltpu.make_async_copy(
            res_hbm.at[:, columns_of(me, k)],
            rbuf.at[quad, :, pl.ds(k * share, share)],
            local_sems.at[3 + k],
        )
        for k in range(4)
    ]
    for copy in locals_:
        copy.start()
    for k in range(GROUP):
        pltpu.make_async_copy(
            head_hbm.at[:, pl.ds(k * share, share)],
            head.at[:, pl.ds(((k // 8 * 2 + k % 2) * 4 + k // 2 % 4) * share, share)],
            head_sem,
        ).start()
    idbuf[me] = jnp.broadcast_to(ids[...], (8, 128))

    pl.semaphore_wait(barrier, GROUP - 1 + 3)

    def send_doc(slot, halves, *targets, own=False):
        for half in halves:
            for target in targets:
                dst = dbuf.at[slot, half]
                remote(doc_hbm.at[half] if own else dst, dst, dp_send, dp_recv.at[slot, half], dp=target)

    def wait_doc(slot, half):
        arrived(dbuf.at[slot, half], dp_recv.at[slot, half])

    send_doc(row, (0, 1), *near_rows, own=True)

    quad_peers = (device(1, 0, 0), device(0, 0, 1), device(1, 0, 1))
    remote(q_hbm, qbuf.at[x], q_send, q_recv, fsdp=device(1, 0, 0))

    w_rows = wbuf.shape[2] // PIECES

    def w_at(slot, half, p):
        return wbuf.at[slot, half, pl.ds(p * w_rows, w_rows)]

    def send_w(slot, half, p, *targets, own=False):
        dst = w_at(slot, half, p)
        src = w_hbm.at[half, pl.ds(p * w_rows, w_rows)] if own else dst
        for target in targets:
            remote(src, dst, w_send, w_recv.at[slot, half, p], fsdp=target)

    def wait_w(slot, half, p):
        arrived(w_at(slot, half, p), w_recv.at[slot, half, p])

    zp, zm = (z + 1) % 4, (z + 3) % 4

    @pl.loop(0, PIECES)
    def _(p):
        send_w(z, 0, p, device(0, 1, 0), own=True)
        send_w(z, 1, p, device(0, 3, 0), own=True)

    partner, up, down = doc_row(1, 0), doc_row(0, 1), doc_row(0, 3)
    for half in range(2):
        wait_doc(partner, half)
        send_doc(partner, (half,), up, down)

    for dh in range(2):
        wait_doc(doc_row(dh, 3), 0)
        send_doc(doc_row(dh, 3), (0,), up)
        wait_doc(doc_row(dh, 1), 1)
        send_doc(doc_row(dh, 1), (1,), down)

    @pl.loop(0, PIECES)
    def _(p):
        wait_w(zm, 0, p)
        send_w(zm, 0, p, device(0, 1, 0))
        wait_w(zp, 1, p)
        send_w(zp, 1, p, device(0, 3, 0))

    for dh in range(2):
        wait_doc(doc_row(dh, 3), 1)
        wait_doc(doc_row(dh, 1), 0)
        for half in range(2):
            wait_doc(doc_row(dh, 2), half)
    locals_[0].wait()

    half_width = kv.shape[3]
    for g in range(2):
        for half in range(2):
            kv[me, half * 2 + g] = dbuf[source[row], half, :, g * half_width : (g + 1) * half_width]

    def kv_view(slot, p):
        return kv.at[slot, p]

    groups = []
    for g in range(2):
        groups.append(
            Gather(me, kv_view, lambda p: kv.at[me, p], kv_send, kv_recv, (g, g + 1), (2 + g, 3 + g))
        )
    for group in groups:
        group.wave1()
    for wave in (Gather.wave2, Gather.wave3, Gather.wave4, Gather.wave5):
        for group in groups:
            wave(group)
    for other in quad_peers:
        for k in range(4):
            remote(
                res_hbm.at[:, columns_of(other, k)],
                rbuf.at[quad, :, pl.ds(k * share, share)],
                r_send,
                r_recv.at[quad],
                fsdp=other,
            )

    @pl.loop(1, GROUP)
    def _(j):
        remote(idbuf.at[me], idbuf.at[me], id_send, id_recv.at[me], fsdp=(me + j) % GROUP)


    @pl.loop(0, PIECES)
    def _(p):
        send_w(z, 1, p, device(0, 1, 0), own=True)
        send_w(z, 0, p, device(0, 3, 0), own=True)

    locals_[1].wait()
    arrived(qbuf.at[1 - x], q_recv)

    for g in range(2):
        groups[g].last(0, 4)

        @pl.loop(0, GROUP // 2)
        def _(k):
            for half in range(2):
                groups[g].wait(2 * k + 1 - core, half * 2 + g)

        @pl.loop(0, HEADS // 2, unroll=4)
        def _(h):
            columns = pl.ds(pl.multiple_of(h * DEPTH, DEPTH), DEPTH)
            whole = pl.ds(pl.multiple_of(h * DEPTH + g * half_width, DEPTH), DEPTH)
            keys = kv[:, g, :, columns].reshape(-1, DEPTH)
            values = kv[:, 2 + g, :, columns].reshape(-1, DEPTH)
            scores = lax.dot_general(
                qbuf[:, :, whole].reshape(-1, DEPTH),
                keys,
                (((1,), (1,)), ((), ())),
                preferred_element_type=jnp.float32,
            ) * float(DEPTH) ** (-0.5)
            raised = jnp.exp(scores - jnp.max(scores, axis=1, keepdims=True))
            weights = (raised / jnp.sum(raised, axis=1, keepdims=True)).astype(jnp.bfloat16)
            mixed = jnp.dot(weights, values, preferred_element_type=jnp.float32).astype(jnp.bfloat16)
            att[core, :, :, whole] = mixed.reshape(2, tokens, DEPTH)

        done = att.at[core, :, :, pl.ds(g * half_width, half_width)]
        remote(done, done, att_send, att_recv.at[g], fsdp=device(0, 0, 1))

    for copy in locals_[2:]:
        copy.wait()

    @pl.loop(0, PIECES)
    def _(p):
        wait_w(zp, 0, p)
        wait_w(zm, 1, p)
        wait_w((z + 2) % 4, 0, p)
        wait_w((z + 2) % 4, 1, p)

    for other in quad_peers:
        slot = (other // 8) * 2 + other % 2
        arrived(rbuf.at[slot], r_recv.at[slot])
    for g in range(2):
        arrived(att.at[1 - core, :, :, pl.ds(g * half_width, half_width)], att_recv.at[g])

    def project(k, squares):
        columns = pl.ds(pl.multiple_of(k * share, share), share)
        weight = wbuf[k].reshape(-1, share)
        mixed = jnp.dot(att[...].reshape(4 * tokens, -1), weight, preferred_element_type=jnp.float32)
        out = []
        for slot in range(4):
            start = ((slot % 2) * 2 + slot // 2) * tokens
            part = mixed[start : start + tokens] + rbuf[slot, :, columns].astype(jnp.float32)
            summed[slot, :, columns] = part
            out.append(squares[slot] + part * part)
        return tuple(out)

    zero = jnp.zeros((tokens, share), jnp.float32)
    squares = lax.fori_loop(0, 4, project, (zero,) * 4)
    for slot in range(4):
        own = jnp.sum(squares[slot], axis=1, keepdims=True)
        sq_out[slot] = jnp.broadcast_to(own, (tokens, 128)).T[0:8]
    for other in quad_peers:
        remote(sq_out, sq_in.at[quad], sq_send, sq_recv.at[quad], fsdp=other)
    sq_in[quad] = sq_out[...]
    for other in quad_peers:
        slot = (other // 8) * 2 + other % 2
        arrived(sq_in.at[slot], sq_recv.at[slot])
    mean = (sq_in[0] + sq_in[1] + sq_in[2] + sq_in[3]) / head_hbm.shape[1]
    scale = lax.rsqrt(mean + 1e-06)
    for slot in range(4):
        factor = jnp.broadcast_to(scale[slot, 0:1], (128, tokens)).T[:, 0:1]
        for k in range(4):
            columns = pl.ds(k * share, share)
            hidden = summed[slot, :, columns] * factor * gain[:, columns_of(me, k)]
            spot = pl.ds(pl.multiple_of((quad * 4 + k) * share, share), share)
            rows = pl.ds((slot // 2) * 2 * tokens + (slot % 2) * tokens, tokens)
            hbuf[z, rows, spot] = hidden.astype(jnp.bfloat16)

    piece = hbuf.shape[1] // HIDDEN
    quarter = hbuf.shape[2] // 4

    def hidden_view(slot, p):
        place = (slot // 8) * 2 + slot % 2
        return hbuf.at[
            (slot // 2) % 4,
            pl.ds(p * piece, piece),
            pl.ds(pl.multiple_of(place * quarter, quarter), quarter),
        ]

    hg = Gather(
        me, hidden_view, lambda p: hidden_view(me, p), h_send, h_recv, (0, VIA_X), (VIA_X, HIDDEN)
    )
    hg.wave1()
    arrived(head, head_sem)

    @pl.loop(1, GROUP)
    def _(j):
        other = (me + j) % GROUP
        arrived(idbuf.at[other], id_recv.at[other])

    vocab = lax.broadcasted_iota(jnp.int32, (head.shape[0], 128), 0) + me * head.shape[0]

    parts = HIDDEN // 4

    def finish(spot, start, count):
        rows = pl.ds(start, count * tokens)
        logits[:, : count * tokens] = lax.dot_general(
            head[...], hbuf[spot, rows], (((1,), (1,)), ((), ())), preferred_element_type=jnp.float32
        )
        for c in range(count):
            index = start // tokens + c
            slot = (index // 2) * 8 + spot * 2 + index % 2
            block = logits[:, c * tokens : (c + 1) * tokens]
            largest = jnp.max(block, axis=0, keepdims=True)
            total = jnp.sum(jnp.exp(block - largest), axis=0, keepdims=True)
            picked = jnp.sum(jnp.where(vocab == idbuf[slot][0:1], block, 0.0), axis=0, keepdims=True)
            stat_out[slot, 0:1] = largest
            stat_out[slot, 1:2] = total
            stat_out[slot, 2:3] = picked
            stat_out[slot, 3:8] = jnp.zeros((5, tokens), jnp.float32)

            @pl.when(slot != me)
            def _():
                remote(stat_out.at[slot], stat_in.at[me], stat_send, stat_recv.at[me], fsdp=slot)

    def wait_other_core(spot, low, high):
        for dx in range(2):
            slot = dx * 8 + spot * 2 + 1 - core
            pl.loop(low, high)(lambda p: hg.wait(slot, p))

    @pl.loop(0, 6)
    def _(step):
        for when, wave in ((0, hg.wave2), (1, hg.wave3), (2, hg.wave4), (4, hg.wave5)):
            pl.when(step == when)(wave)
        half = jnp.where(step < 2, step, (step - 2) // 2)
        dz = jnp.where(step < 2, 0, 1 + 2 * (step % 2))
        spot = (z + dz) % 4
        wait_other_core(spot, half * 2 * parts, half * 2 * parts + 2 * parts)
        finish(spot, half * 2 * tokens, 2)

    def last_quarter(step):
        quarter_of = (step % 2) * 2 + step // 2
        for k in range(4):
            pl.when(quarter_of == k)(lambda: hg.last(k * parts, (k + 1) * parts))
        wait_other_core(spot, quarter_of * parts, quarter_of * parts + parts)
        finish(spot, quarter_of * tokens, 1)

    spot = (z + 2) % 4
    pl.loop(0, 4)(last_quarter)

    stat_in[me] = stat_out[me]

    @pl.loop(1, GROUP)
    def _(j):
        other = (me + j) % GROUP
        arrived(stat_in.at[other], stat_recv.at[other])

    largest = stat_in[:, 0, :]
    highest = jnp.max(largest, axis=0, keepdims=True)
    total = jnp.sum(stat_in[:, 1, :] * jnp.exp(largest - highest), axis=0, keepdims=True)
    picked = jnp.sum(stat_in[:, 2, :], axis=0, keepdims=True)
    new = picked - (highest + jnp.log(total))
    position = core * tokens + lax.broadcasted_iota(jnp.int32, (1, 128), 1)
    live = position < lengths[0, me // 2]
    before = old[...]
    ratio_out[...] = jnp.where(live, new - before, 0.0)
    gap = jnp.clip(before - new, -3.0, 3.0)
    kl_out[...] = jnp.where(live, jnp.exp(gap) - gap - 1.0, 0.0)

    arrived(hbuf.at[:, pl.ds(0, 15 * hbuf.shape[1] // 16)], h_send)
    for buf, count, sem in (
        (kv, 15, kv_send),
        (wbuf, 3, w_send),
        (dbuf, 7, dp_send),
        (rbuf, 3, r_send),
        (qbuf, 1, q_send),
        (att, 1, att_send),
        (sq_in, 3, sq_send),
        (idbuf, 15, id_send),
        (stat_out, 15, stat_send),
    ):
        view = buf.at[pl.ds(0, count)]
        arrived(view, sem)


def on_device(
    queries, doc_kv, residual, out_weight, out_gain, head, source, lengths, sampled, old_logprob
):
    tokens, width = queries.shape
    columns = residual.shape[1]
    share = out_weight.shape[1]
    positions = doc_kv.shape[2]
    bf16, f32 = jnp.bfloat16, jnp.float32
    smem = pl.BlockSpec(memory_space=pltpu.SMEM)
    vmem = pl.BlockSpec(memory_space=pltpu.VMEM)
    any_ = pl.BlockSpec(memory_space=pl.ANY)
    dma = pltpu.SemaphoreType.DMA
    out = jax.ShapeDtypeStruct((1, tokens), f32)
    ratio, kl = pl.pallas_call(
        kernel,
        out_shape=(out, out),
        in_specs=[smem, smem, vmem, vmem, vmem] + [any_] * 5,
        out_specs=(vmem, vmem),
        scratch_shapes=[
            pltpu.VMEM(head.shape, bf16),
            pltpu.VMEM((4, 2, width // 2, share), bf16),
            pltpu.VMEM((4, 4 * tokens, columns), bf16),
            pltpu.VMEM((ROWS, 2, positions, width), bf16),
            pltpu.VMEM((GROUP, 4, positions, width // 2), bf16),
            pltpu.VMEM((2, tokens, width), bf16),
            pltpu.VMEM((4, tokens, columns // 4), bf16),
            pltpu.VMEM((2, 2, tokens, width), bf16),
            pltpu.VMEM((4, tokens, columns // 4), f32),
            pltpu.VMEM((head.shape[0], 256), f32),
            pltpu.VMEM((GROUP, 8, 128), jnp.int32),
            pltpu.VMEM((4, 8, 128), f32),
            pltpu.VMEM((4, 4, 8, 128), f32),
            pltpu.VMEM((GROUP, 8, 128), f32),
            pltpu.VMEM((GROUP, 8, 128), f32),
            dma((7,)),
            dma,
            dma,
            dma((4, 2, PIECES)),
            dma,
            dma((GROUP, HIDDEN)),
            dma,
            dma((GROUP, 4)),
            dma,
            dma((ROWS, 2)),
            dma,
            dma,
            dma,
            dma((4,)),
            dma,
            dma((2,)),
            dma,
            dma((4,)),
            dma,
            dma((GROUP,)),
            dma,
            dma((GROUP,)),
        ],
        compiler_params=pltpu.CompilerParams(
            collective_id=0, has_side_effects=True, vmem_limit_bytes=60 * 1024 * 1024
        ),
    )(
        source,
        lengths,
        sampled.reshape(1, tokens),
        old_logprob.reshape(1, tokens),
        out_gain.reshape(1, columns),
        queries,
        doc_kv.reshape(2, positions, width),
        residual,
        out_weight.reshape(2, width // 2, share),
        head,
    )
    return ratio.reshape(tokens), kl.reshape(tokens)


def solution(mesh):
    return jax.shard_map(
        on_device,
        mesh=mesh,
        in_specs=(
            P(("dp", "fsdp"), None),
            P(None, "dp", "fsdp", None),
            P(("dp", "fsdp"), None),
            P(None, "fsdp"),
            P(),
            P("fsdp", None),
            P(),
            P("dp", None),
            P(("dp", "fsdp")),
            P(("dp", "fsdp")),
        ),
        out_specs=(P(("dp", "fsdp")), P(("dp", "fsdp"))),
        check_vma=False,
    )
```

```python
import jax
import jax.numpy as jnp
from jax import lax
from jax.experimental import pallas as pl
from jax.experimental.pallas import tpu as pltpu
from jax.sharding import PartitionSpec as P

HEADS = 8
DEPTH = 256
GROUP = 16
ROWS = 8
MESH = pl.DeviceIdType.MESH
PIECES = 4
HIDDEN = 16
VIA_X = 9


class Gather:
    def __init__(self, me, view, own, send_sem, recv_sem, first, second):
        self.me, self.view, self.own = me, view, own
        self.send_sem, self.recv_sem = send_sem, recv_sem
        self.first, self.second = first, second
        self.middle = (second[0] + second[1] + 1) // 2
        x, z, core = me // 8, (me // 2) % 4, me % 2

        def slot(dx, dz):
            return ((x + dx) % 2) * 8 + ((z + dz) % 4) * 2 + core

        self.x, self.zp, self.zm, self.z2 = slot(1, 0), slot(0, 1), slot(0, 3), slot(0, 2)
        self.xzp, self.xzm, self.xz2 = slot(1, 1), slot(1, 3), slot(1, 2)
        self.core = me + 1 - 2 * core

    def send(self, slot, p, *targets, own=False):
        dst = self.view(slot, p)
        src = self.own(p) if own else dst
        for target in targets:
            pltpu.make_async_remote_copy(
                src_ref=src,
                dst_ref=dst,
                send_sem=self.send_sem,
                recv_sem=self.recv_sem.at[slot, p],
                device_id={"fsdp": target},
                device_id_type=MESH,
            ).start()

    def wait(self, slot, p):
        view = self.view(slot, p)
        pltpu.make_async_copy(view, view, self.recv_sem.at[slot, p]).wait()

    def pass_on(self, slot, p, *targets):
        self.wait(slot, p)
        self.send(slot, p, *targets, self.core)

    def each(self, low, high, step):
        if high - low == 1:
            step(low)
        elif high > low:
            pl.loop(low, high)(step)

    def wave1(self, low=0, high=1 << 10):
        first = max(low, self.first[0]), min(high, self.first[1])
        second = max(low, self.second[0]), min(high, self.second[1])
        self.each(*first, lambda p: self.send(self.me, p, self.x, own=True))
        self.each(*second, lambda p: self.send(self.me, p, self.zp, self.zm, own=True))
        self.each(*first, lambda p: self.send(self.me, p, self.zp, self.zm, self.core, own=True))
        self.each(*second, lambda p: self.send(self.me, p, self.x, self.core, own=True))

    def wave2(self):
        self.each(*self.first, lambda p: self.pass_on(self.x, p, self.zp, self.zm))

    def wave3(self):
        def up(p):
            self.pass_on(self.zp, p, self.x)
            self.pass_on(self.zm, p, self.zp, self.x)

        def down(p):
            self.pass_on(self.zp, p, self.zm, self.x)
            self.pass_on(self.zm, p, self.x)

        def own_side(p):
            self.pass_on(self.zm, p, self.zp)
            self.pass_on(self.zp, p)

        self.each(self.middle, self.second[1], up)
        self.each(self.second[0], self.middle, down)
        self.each(*self.first, own_side)
        self.each(*self.second, lambda p: self.pass_on(self.x, p))

    def wave4(self):
        def far_side(p):
            self.pass_on(self.xzp, p, self.zm)
            self.pass_on(self.xzm, p)

        self.each(*self.first, far_side)

    def wave5(self):
        def far_side(p):
            self.pass_on(self.xzp, p)
            self.pass_on(self.xzm, p)

        self.each(*self.second, lambda p: self.pass_on(self.z2, p, self.x))
        self.each(*self.second, far_side)

    def last(self, low, high):
        def step(p):
            self.pass_on(self.z2, p)
            self.pass_on(self.xz2, p)

        self.each(max(low, self.first[0]), min(high, self.first[1]), step)
        self.each(
            max(low, self.second[0]), min(high, self.second[1]), lambda p: self.pass_on(self.xz2, p)
        )


def kernel(
    source,
    lengths,
    ids,
    old,
    gain,
    q_hbm,
    doc_hbm,
    res_hbm,
    w_hbm,
    head_hbm,
    ratio_out,
    kl_out,
    head,
    wbuf,
    hbuf,
    doc_a,
    doc_b,
    kv,
    qbuf,
    rbuf,
    att,
    summed,
    logits,
    idbuf,
    sq_out,
    sq_in,
    stat_out,
    stat_in,
    local_sems,
    head_sem,
    w_send,
    w_recv,
    ws_send,
    ws_recv,
    h_send,
    h_recv,
    kv_send,
    kv_recv,
    dp_send,
    dp_recv,
    q_send,
    q_recv,
    r_send,
    r_recv,
    att_send,
    att_recv,
    sq_send,
    sq_recv,
    id_send,
    id_recv,
    stat_send,
    stat_recv,
):
    row = lax.axis_index("dp")
    me = lax.axis_index("fsdp")
    x, z, core = me // 8, (me // 2) % 4, me % 2
    xh, y = row // 4, row % 4
    quad = x * 2 + core
    share = wbuf.shape[3]
    tokens = qbuf.shape[1]

    def device(dx, dz, dc):
        return ((x + dx) % 2) * 8 + ((z + dz) % 4) * 2 + (core + dc) % 2

    def doc_row(dh, dy):
        return ((xh + dh) % 2) * 4 + (y + dy) % 4

    def columns_of(other, k):
        block = (other // 8) * 8 + k * 2 + other % 2
        return pl.ds(pl.multiple_of(block * share, share), share)

    def remote(src, dst, send, recv, **where):
        pltpu.make_async_remote_copy(
            src_ref=src, dst_ref=dst, send_sem=send, recv_sem=recv, device_id=where, device_id_type=MESH
        ).start()

    def arrived(view, sem):
        pltpu.make_async_copy(view, view, sem).wait()

    barrier = pltpu.get_barrier_semaphore()

    @pl.loop(1, GROUP)
    def _(j):
        pl.semaphore_signal(barrier, inc=1, device_id={"fsdp": (me + j) % GROUP}, device_id_type=MESH)

    near_rows = (doc_row(1, 0), doc_row(0, 1), doc_row(0, 3))
    for other in near_rows:
        pl.semaphore_signal(barrier, inc=1, device_id={"dp": other}, device_id_type=MESH)

    half_width = kv.shape[3]

    def doc_piece(p):
        return doc_hbm.at[p % 2, :, pl.ds(p // 2 * half_width, half_width)]

    def doc_view(slot, p):
        return (doc_a, doc_b)[p // 2].at[slot, p % 2]

    locals_ = [
        pltpu.make_async_copy(q_hbm, qbuf.at[x], local_sems.at[0]),
        pltpu.make_async_copy(w_hbm, wbuf.at[z], local_sems.at[1]),
    ] + [
        pltpu.make_async_copy(
            res_hbm.at[:, columns_of(me, k)],
            rbuf.at[quad, :, pl.ds(k * share, share)],
            local_sems.at[2 + k],
        )
        for k in range(4)
    ]
    doc_locals = [
        pltpu.make_async_copy(doc_piece(p), doc_view(row, p), local_sems.at[6 + p]) for p in range(4)
    ]
    for copy in doc_locals + locals_:
        copy.start()
    for k in range(GROUP):
        pltpu.make_async_copy(
            head_hbm.at[:, pl.ds(k * share, share)],
            head.at[:, pl.ds(((k // 8 * 2 + k % 2) * 4 + k // 2 % 4) * share, share)],
            head_sem,
        ).start()
    idbuf[me] = jnp.broadcast_to(ids[...], (8, 128))

    pl.semaphore_wait(barrier, GROUP - 1 + 3)

    quad_peers = (device(1, 0, 0), device(0, 0, 1), device(1, 0, 1))
    partner, up, down = near_rows

    def send_row(view, sems, slot, p, *targets, src=None):
        dst = view(slot, p)
        for target in targets:
            remote(dst if src is None else src, dst, sems[0], sems[1].at[slot, p], dp=target)

    def wait_row(view, sems, slot, p):
        arrived(view(slot, p), sems[1].at[slot, p])

    def relay(view, sems, low, high):
        for dh in range(2):
            wait_row(view, sems, doc_row(dh, 3), low)
            send_row(view, sems, doc_row(dh, 3), low, up)
            wait_row(view, sems, doc_row(dh, 1), high)
            send_row(view, sems, doc_row(dh, 1), high, down)

    def wait_rest(view, sems, low, high):
        for dh in range(2):
            wait_row(view, sems, doc_row(dh, 3), high)
            wait_row(view, sems, doc_row(dh, 1), low)
            wait_row(view, sems, doc_row(dh, 2), low)
            wait_row(view, sems, doc_row(dh, 2), high)

    doc = (doc_view, (dp_send, dp_recv))

    for p in range(4):
        send_row(*doc, row, p, partner, up, down, src=doc_piece(p))
    remote(q_hbm, qbuf.at[x], q_send, q_recv, fsdp=device(1, 0, 0))

    w_rows = wbuf.shape[2] // PIECES
    eighth = wbuf.shape[2] // 8
    above, far, below = (z + 1) % 4, (z + 2) % 4, (z + 3) % 4

    def send_w(half, p, target):
        rows = pl.ds(p * w_rows, w_rows)
        remote(
            w_hbm.at[half, rows], wbuf.at[z, half, rows], w_send, w_recv.at[half, p], fsdp=target
        )

    def part_view(slot, p):
        owner = (far, far, below, above)[p]
        return wbuf.at[owner, (0, 1, 1, 0)[p], pl.ds(slot * eighth, eighth)]

    part = (part_view, (ws_send, ws_recv))

    for p in range(4):
        rows = pl.ds(row * eighth, eighth)
        half = (0, 1, 1, 0)[p]
        remote(
            w_hbm.at[half, rows],
            wbuf.at[z, half, rows],
            ws_send,
            ws_recv.at[row, p],
            fsdp=device(0, (2, 2, 1, 3)[p], 0),
        )

    @pl.loop(0, PIECES)
    def _(p):
        send_w(0, p, device(0, 1, 0))
        send_w(1, p, device(0, 3, 0))

    for p in (0, 1):
        wait_row(*doc, partner, p)
        send_row(*doc, partner, p, up, down)
    relay(*doc, 0, 1)
    for p in (2, 3):
        wait_row(*doc, partner, p)
        send_row(*doc, partner, p, up, down)

    def kv_view(slot, p):
        return kv.at[slot, p]

    groups = []
    for g in range(2):
        groups.append(
            Gather(
                me,
                kv_view,
                lambda p: kv.at[me, p],
                kv_send,
                kv_recv,
                (2 * g, 2 * g + 2),
                (2 * g + 2, 2 * g + 2),
            )
        )

    def choose(g):
        wait_rest(*doc, 2 * g, 2 * g + 1)
        for p in (2 * g, 2 * g + 1):
            doc_locals[p].wait()
        kv[me, pl.ds(2 * g, 2)] = (doc_a, doc_b)[g][source[row]]
        groups[g].wave1()

    def attend(g):
        groups[g].last(0, 4)

        @pl.loop(0, GROUP // 2)
        def _(k):
            for half in range(2):
                groups[g].wait(2 * k + 1 - core, 2 * g + half)

        @pl.loop(0, HEADS // 2, unroll=4)
        def _(h):
            columns = pl.ds(pl.multiple_of(h * DEPTH, DEPTH), DEPTH)
            whole = pl.ds(pl.multiple_of(h * DEPTH + g * half_width, DEPTH), DEPTH)
            keys = kv[:, 2 * g, :, columns].reshape(-1, DEPTH)
            values = kv[:, 2 * g + 1, :, columns].reshape(-1, DEPTH)
            scores = lax.dot_general(
                qbuf[:, :, whole].reshape(-1, DEPTH),
                keys,
                (((1,), (1,)), ((), ())),
                preferred_element_type=jnp.float32,
            ) * float(DEPTH) ** (-0.5)
            raised = jnp.exp(scores - jnp.max(scores, axis=1, keepdims=True))
            weights = (raised / jnp.sum(raised, axis=1, keepdims=True)).astype(jnp.bfloat16)
            mixed = jnp.dot(weights, values, preferred_element_type=jnp.float32).astype(jnp.bfloat16)
            att[core, :, :, whole] = mixed.reshape(2, tokens, DEPTH)

        done = att.at[core, :, :, pl.ds(g * half_width, half_width)]
        remote(done, done, att_send, att_recv.at[g], fsdp=device(0, 0, 1))

    choose(0)
    relay(*doc, 2, 3)
    for p in range(4):
        wait_row(*part, row, p)
        send_row(*part, row, p, partner, up, down)
    groups[0].wave2()
    groups[0].wave3()
    choose(1)
    for other in quad_peers:
        for k in range(4):
            remote(
                res_hbm.at[:, columns_of(other, k)],
                rbuf.at[quad, :, pl.ds(k * share, share)],
                r_send,
                r_recv.at[quad],
                fsdp=other,
            )

    groups[0].wave4()
    groups[0].wave5()
    groups[1].wave2()
    groups[1].wave3()
    for p in range(4):
        wait_row(*part, partner, p)
        send_row(*part, partner, p, up, down)
    locals_[0].wait()
    arrived(qbuf.at[1 - x], q_recv)
    attend(0)
    groups[1].wave4()
    groups[1].wave5()
    relay(*part, 0, 1)
    relay(*part, 2, 3)
    @pl.loop(1, GROUP)
    def _(j):
        remote(idbuf.at[me], idbuf.at[me], id_send, id_recv.at[me], fsdp=(me + j) % GROUP)


    attend(1)

    for copy in locals_[1:]:
        copy.wait()

    @pl.loop(0, PIECES)
    def _(p):
        rows = pl.ds(p * w_rows, w_rows)
        arrived(wbuf.at[below, 0, rows], w_recv.at[0, p])
        arrived(wbuf.at[above, 1, rows], w_recv.at[1, p])

    wait_rest(*part, 0, 1)
    wait_rest(*part, 2, 3)

    for other in quad_peers:
        slot = (other // 8) * 2 + other % 2
        arrived(rbuf.at[slot], r_recv.at[slot])
    for g in range(2):
        arrived(att.at[1 - core, :, :, pl.ds(g * half_width, half_width)], att_recv.at[g])

    piece = 2 * hbuf.shape[2] // HIDDEN
    quarter = hbuf.shape[3] // 4

    def hidden_view(slot, p):
        place = (slot // 8) * 2 + slot % 2
        return hbuf.at[
            (slot // 2) % 4,
            p // (HIDDEN // 2),
            pl.ds(p % (HIDDEN // 2) * piece, piece),
            pl.ds(pl.multiple_of(place * quarter, quarter), quarter),
        ]

    hg = Gather(
        me, hidden_view, lambda p: hidden_view(me, p), h_send, h_recv, (0, VIA_X), (VIA_X, HIDDEN)
    )
    def project(chip):
        def step(k, squares):
            columns = pl.ds(pl.multiple_of(k * share, share), share)
            weight = wbuf[k].reshape(-1, share)
            mixed = jnp.dot(
                att[:, chip].reshape(2 * tokens, -1), weight, preferred_element_type=jnp.float32
            )
            base = jnp.concatenate([rbuf[2 * chip + c, :, columns] for c in range(2)])
            total = mixed + base.astype(jnp.float32)
            summed[chip, :, columns] = total
            return squares + total * total

        squares = lax.fori_loop(0, 4, step, jnp.zeros((2 * tokens, share), jnp.float32))
        own = jnp.sum(squares, axis=1, keepdims=True)
        sq_out[chip] = jnp.broadcast_to(own, (2 * tokens, 128)).T[0:8]
        for other in quad_peers:
            remote(
                sq_out.at[chip], sq_in.at[chip, quad], sq_send, sq_recv.at[chip, quad], fsdp=other
            )
        sq_in[chip, quad] = sq_out[chip]

    def normalize(chip):
        for other in quad_peers:
            slot = (other // 8) * 2 + other % 2
            arrived(sq_in.at[chip, slot], sq_recv.at[chip, slot])
        mean = jnp.sum(sq_in[chip, :, 0:1], axis=0) / head_hbm.shape[1]
        scale = lax.rsqrt(mean + 1e-06)
        factor = jnp.broadcast_to(scale, (128, 2 * tokens)).T[:, 0:1]
        for k in range(4):
            columns = pl.ds(k * share, share)
            hidden = summed[chip, :, columns] * factor * gain[:, columns_of(me, k)]
            spot = pl.ds(pl.multiple_of((quad * 4 + k) * share, share), share)
            hbuf[z, chip, :, spot] = hidden.astype(jnp.bfloat16)
        hg.wave1(chip * HIDDEN // 2, (chip + 1) * HIDDEN // 2)

    project(0)
    project(1)
    normalize(0)
    normalize(1)
    arrived(head, head_sem)

    @pl.loop(1, GROUP)
    def _(j):
        other = (me + j) % GROUP
        arrived(idbuf.at[other], id_recv.at[other])

    vocab = lax.broadcasted_iota(jnp.int32, (head.shape[0], 128), 0) + me * head.shape[0]

    parts = HIDDEN // 4

    def finish(rows, slots):
        logits[...] = lax.dot_general(
            head[...], rows, (((1,), (1,)), ((), ())), preferred_element_type=jnp.float32
        )
        for c in range(2):
            slot = slots[c]
            block = logits[:, c * tokens : (c + 1) * tokens]
            largest = jnp.max(block, axis=0, keepdims=True)
            total = jnp.sum(jnp.exp(block - largest), axis=0, keepdims=True)
            picked = jnp.sum(jnp.where(vocab == idbuf[slot][0:1], block, 0.0), axis=0, keepdims=True)
            stat_out[slot, 0:1] = largest
            stat_out[slot, 1:2] = total
            stat_out[slot, 2:3] = picked
            stat_out[slot, 3:8] = jnp.zeros((5, tokens), jnp.float32)

            @pl.when(slot != me)
            def _():
                remote(stat_out.at[slot], stat_in.at[me], stat_send, stat_recv.at[me], fsdp=slot)

    def wait_other_core(spot, low, high):
        for dx in range(2):
            slot = dx * 8 + spot * 2 + 1 - core
            pl.loop(low, high)(lambda p: hg.wait(slot, p))

    @pl.loop(0, 6)
    def _(step):
        for when, wave in ((0, hg.wave2), (1, hg.wave3), (2, hg.wave4), (4, hg.wave5)):
            pl.when(step == when)(wave)
        chip = jnp.where(step < 2, step, (step - 2) // 2)
        dz = jnp.where(step < 2, 0, 1 + 2 * (step % 2))
        spot = (z + dz) % 4
        wait_other_core(spot, chip * 2 * parts, chip * 2 * parts + 2 * parts)
        slot = chip * 8 + spot * 2
        finish(hbuf[spot, chip], (slot, slot + 1))

    spot = (z + 2) % 4

    @pl.loop(0, 2)
    def _(c):
        for k in range(2):

            @pl.when(c == k)
            def _():
                hg.last(k * parts, k * parts + parts)
                hg.last((2 + k) * parts, (3 + k) * parts)

        wait_other_core(spot, c * parts, c * parts + parts)
        wait_other_core(spot, (2 + c) * parts, (2 + c) * parts + parts)
        rows = hbuf[spot, :, pl.ds(pl.multiple_of(c * tokens, tokens), tokens)]
        finish(rows.reshape(2 * tokens, -1), (spot * 2 + c, 8 + spot * 2 + c))

    stat_in[me] = stat_out[me]

    @pl.loop(1, GROUP)
    def _(j):
        other = (me + j) % GROUP
        arrived(stat_in.at[other], stat_recv.at[other])

    largest = stat_in[:, 0, :]
    highest = jnp.max(largest, axis=0, keepdims=True)
    total = jnp.sum(stat_in[:, 1, :] * jnp.exp(largest - highest), axis=0, keepdims=True)
    picked = jnp.sum(stat_in[:, 2, :], axis=0, keepdims=True)
    new = picked - (highest + jnp.log(total))
    position = core * tokens + lax.broadcasted_iota(jnp.int32, (1, 128), 1)
    live = position < lengths[0, me // 2]
    before = old[...]
    ratio_out[...] = jnp.where(live, new - before, 0.0)
    gap = jnp.clip(before - new, -3.0, 3.0)
    kl_out[...] = jnp.where(live, jnp.exp(gap) - gap - 1.0, 0.0)

    arrived(sq_in.at[:, pl.ds(0, 3)], sq_send)
    arrived(hbuf.at[:, :, pl.ds(0, 15 * hbuf.shape[2] // 16)], h_send)
    for buf, count, sem in (
        (kv, 15, kv_send),
        (wbuf, 1, w_send),
        (wbuf, 2, ws_send),
        (kv, 7, dp_send),
        (rbuf, 3, r_send),
        (qbuf, 1, q_send),
        (att, 1, att_send),
        (idbuf, 15, id_send),
        (stat_out, 15, stat_send),
    ):
        view = buf.at[pl.ds(0, count)]
        arrived(view, sem)


def on_device(
    queries, doc_kv, residual, out_weight, out_gain, head, source, lengths, sampled, old_logprob
):
    tokens, width = queries.shape
    columns = residual.shape[1]
    share = out_weight.shape[1]
    positions = doc_kv.shape[2]
    bf16, f32 = jnp.bfloat16, jnp.float32
    smem = pl.BlockSpec(memory_space=pltpu.SMEM)
    vmem = pl.BlockSpec(memory_space=pltpu.VMEM)
    any_ = pl.BlockSpec(memory_space=pl.ANY)
    dma = pltpu.SemaphoreType.DMA
    out = jax.ShapeDtypeStruct((1, tokens), f32)
    ratio, kl = pl.pallas_call(
        kernel,
        out_shape=(out, out),
        in_specs=[smem, smem, vmem, vmem, vmem] + [any_] * 5,
        out_specs=(vmem, vmem),
        scratch_shapes=[
            pltpu.VMEM(head.shape, bf16),
            pltpu.VMEM((4, 2, width // 2, share), bf16),
            pltpu.VMEM((4, 2, 2 * tokens, columns), bf16),
            pltpu.VMEM((ROWS, 2, positions, width // 2), bf16),
            pltpu.VMEM((ROWS, 2, positions, width // 2), bf16),
            pltpu.VMEM((GROUP, 4, positions, width // 2), bf16),
            pltpu.VMEM((2, tokens, width), bf16),
            pltpu.VMEM((4, tokens, columns // 4), bf16),
            pltpu.VMEM((2, 2, tokens, width), bf16),
            pltpu.VMEM((2, 2 * tokens, columns // 4), f32),
            pltpu.VMEM((head.shape[0], 256), f32),
            pltpu.VMEM((GROUP, 8, 128), jnp.int32),
            pltpu.VMEM((2, 8, 2 * tokens), f32),
            pltpu.VMEM((2, 4, 8, 2 * tokens), f32),
            pltpu.VMEM((GROUP, 8, 128), f32),
            pltpu.VMEM((GROUP, 8, 128), f32),
            dma((10,)),
            dma,
            dma,
            dma((2, PIECES)),
            dma,
            dma((ROWS, 4)),
            dma,
            dma((GROUP, HIDDEN)),
            dma,
            dma((GROUP, 4)),
            dma,
            dma((ROWS, 4)),
            dma,
            dma,
            dma,
            dma((4,)),
            dma,
            dma((2,)),
            dma,
            dma((2, 4)),
            dma,
            dma((GROUP,)),
            dma,
            dma((GROUP,)),
        ],
        compiler_params=pltpu.CompilerParams(
            collective_id=0, has_side_effects=True, vmem_limit_bytes=60 * 1024 * 1024
        ),
    )(
        source,
        lengths,
        sampled.reshape(1, tokens),
        old_logprob.reshape(1, tokens),
        out_gain.reshape(1, columns),
        queries,
        doc_kv.reshape(2, positions, width),
        residual,
        out_weight.reshape(2, width // 2, share),
        head,
    )
    return ratio.reshape(tokens), kl.reshape(tokens)


def solution(mesh):
    return jax.shard_map(
        on_device,
        mesh=mesh,
        in_specs=(
            P(("dp", "fsdp"), None),
            P(None, "dp", "fsdp", None),
            P(("dp", "fsdp"), None),
            P(None, "fsdp"),
            P(),
            P("fsdp", None),
            P(),
            P("dp", None),
            P(("dp", "fsdp")),
            P(("dp", "fsdp")),
        ),
        out_specs=(P(("dp", "fsdp")), P(("dp", "fsdp"))),
        check_vma=False,
    )
```

```python
import jax
import jax.numpy as jnp
from jax import lax
from jax.experimental import pallas as pl
from jax.experimental.pallas import tpu as pltpu
from jax.sharding import PartitionSpec as P

HEADS = 8
DEPTH = 256
GROUP = 16
ROWS = 8
MESH = pl.DeviceIdType.MESH
PIECES = 4
HIDDEN = 16
VIA_X = 9


class Gather:
    def __init__(self, me, view, own, send_sem, recv_sem, first, second):
        self.me, self.view, self.own = me, view, own
        self.send_sem, self.recv_sem = send_sem, recv_sem
        self.first, self.second = first, second
        self.middle = (second[0] + second[1] + 1) // 2
        x, z, core = me // 8, (me // 2) % 4, me % 2

        def slot(dx, dz):
            return ((x + dx) % 2) * 8 + ((z + dz) % 4) * 2 + core

        self.x, self.zp, self.zm, self.z2 = slot(1, 0), slot(0, 1), slot(0, 3), slot(0, 2)
        self.xzp, self.xzm, self.xz2 = slot(1, 1), slot(1, 3), slot(1, 2)
        self.core = me + 1 - 2 * core

    def send(self, slot, p, *targets, own=False):
        dst = self.view(slot, p)
        src = self.own(p) if own else dst
        for target in targets:
            pltpu.make_async_remote_copy(
                src_ref=src,
                dst_ref=dst,
                send_sem=self.send_sem,
                recv_sem=self.recv_sem.at[slot, p],
                device_id={"fsdp": target},
                device_id_type=MESH,
            ).start()

    def wait(self, slot, p):
        view = self.view(slot, p)
        pltpu.make_async_copy(view, view, self.recv_sem.at[slot, p]).wait()

    def pass_on(self, slot, p, *targets):
        self.wait(slot, p)
        self.send(slot, p, *targets, self.core)

    def each(self, low, high, step):
        if high - low == 1:
            step(low)
        elif high > low:
            pl.loop(low, high)(step)

    def wave1(self, low=0, high=1 << 10):
        first = max(low, self.first[0]), min(high, self.first[1])
        second = max(low, self.second[0]), min(high, self.second[1])
        self.each(*first, lambda p: self.send(self.me, p, self.x, own=True))
        self.each(*second, lambda p: self.send(self.me, p, self.zp, self.zm, own=True))
        self.each(*first, lambda p: self.send(self.me, p, self.zp, self.zm, self.core, own=True))
        self.each(*second, lambda p: self.send(self.me, p, self.x, self.core, own=True))

    def wave2(self):
        self.each(*self.first, lambda p: self.pass_on(self.x, p, self.zp, self.zm))

    def wave3(self):
        def up(p):
            self.pass_on(self.zp, p, self.x)
            self.pass_on(self.zm, p, self.zp, self.x)

        def down(p):
            self.pass_on(self.zp, p, self.zm, self.x)
            self.pass_on(self.zm, p, self.x)

        def own_side(p):
            self.pass_on(self.zm, p, self.zp)
            self.pass_on(self.zp, p)

        self.each(self.middle, self.second[1], up)
        self.each(self.second[0], self.middle, down)
        self.each(*self.first, own_side)
        self.each(*self.second, lambda p: self.pass_on(self.x, p))

    def wave4(self):
        def far_side(p):
            self.pass_on(self.xzp, p, self.zm)
            self.pass_on(self.xzm, p)

        self.each(*self.first, far_side)

    def wave5(self):
        def far_side(p):
            self.pass_on(self.xzp, p)
            self.pass_on(self.xzm, p)

        self.each(*self.second, lambda p: self.pass_on(self.z2, p, self.x))
        self.each(*self.second, far_side)

    def last(self, low, high):
        def step(p):
            self.pass_on(self.z2, p)
            self.pass_on(self.xz2, p)

        self.each(max(low, self.first[0]), min(high, self.first[1]), step)
        self.each(
            max(low, self.second[0]), min(high, self.second[1]), lambda p: self.pass_on(self.xz2, p)
        )


def kernel(
    source,
    lengths,
    ids,
    old,
    gain,
    q_hbm,
    doc_hbm,
    res_hbm,
    w_hbm,
    head_hbm,
    out,
    head,
    wbuf,
    hbuf,
    doc_a,
    doc_b,
    kv,
    qbuf,
    rbuf,
    att,
    summed,
    logits,
    idbuf,
    sq_out,
    sq_in,
    stat_out,
    stat_in,
    local_sems,
    head_sem,
    w_send,
    w_recv,
    ws_send,
    ws_recv,
    h_send,
    h_recv,
    kv_send,
    kv_recv,
    dp_send,
    dp_recv,
    q_send,
    q_recv,
    r_send,
    r_recv,
    att_send,
    att_recv,
    sq_send,
    sq_recv,
    id_send,
    id_recv,
    stat_send,
    stat_recv,
):
    row = lax.axis_index("dp")
    me = lax.axis_index("fsdp")
    x, z, core = me // 8, (me // 2) % 4, me % 2
    xh, y = row // 4, row % 4
    quad = x * 2 + core
    share = wbuf.shape[3]
    tokens = qbuf.shape[1]

    def device(dx, dz, dc):
        return ((x + dx) % 2) * 8 + ((z + dz) % 4) * 2 + (core + dc) % 2

    def doc_row(dh, dy):
        return ((xh + dh) % 2) * 4 + (y + dy) % 4

    def columns_of(other, k):
        block = (other // 8) * 8 + k * 2 + other % 2
        return pl.ds(pl.multiple_of(block * share, share), share)

    def remote(src, dst, send, recv, **where):
        pltpu.make_async_remote_copy(
            src_ref=src, dst_ref=dst, send_sem=send, recv_sem=recv, device_id=where, device_id_type=MESH
        ).start()

    def arrived(view, sem):
        pltpu.make_async_copy(view, view, sem).wait()

    barrier = pltpu.get_barrier_semaphore()

    @pl.loop(1, GROUP)
    def _(j):
        pl.semaphore_signal(barrier, inc=1, device_id={"fsdp": (me + j) % GROUP}, device_id_type=MESH)

    near_rows = (doc_row(1, 0), doc_row(0, 1), doc_row(0, 3))
    for other in near_rows:
        pl.semaphore_signal(barrier, inc=1, device_id={"dp": other}, device_id_type=MESH)

    half_width = kv.shape[3]

    def doc_piece(p):
        return doc_hbm.at[p % 2, :, pl.ds(p // 2 * half_width, half_width)]

    def doc_view(slot, p):
        return (doc_a, doc_b)[p // 2].at[slot, p % 2]

    locals_ = [
        pltpu.make_async_copy(q_hbm, qbuf.at[x], local_sems.at[0]),
        pltpu.make_async_copy(w_hbm, wbuf.at[z], local_sems.at[1]),
    ] + [
        pltpu.make_async_copy(
            res_hbm.at[:, columns_of(me, k)],
            rbuf.at[quad, :, pl.ds(k * share, share)],
            local_sems.at[2 + k],
        )
        for k in range(4)
    ]
    doc_locals = [
        pltpu.make_async_copy(doc_piece(p), doc_view(row, p), local_sems.at[6 + p]) for p in range(4)
    ]
    for copy in doc_locals + locals_:
        copy.start()
    for k in range(GROUP):
        pltpu.make_async_copy(
            head_hbm.at[:, pl.ds(k * share, share)],
            head.at[:, pl.ds(((k // 8 * 2 + k % 2) * 4 + k // 2 % 4) * share, share)],
            head_sem,
        ).start()
    idbuf[me] = jnp.broadcast_to(ids[...], (8, 128))

    pl.semaphore_wait(barrier, GROUP - 1 + 3)

    quad_peers = (device(1, 0, 0), device(0, 0, 1), device(1, 0, 1))
    partner, up, down = near_rows

    def send_row(view, sems, slot, p, *targets, src=None):
        dst = view(slot, p)
        for target in targets:
            remote(dst if src is None else src, dst, sems[0], sems[1].at[slot, p], dp=target)

    def wait_row(view, sems, slot, p):
        arrived(view(slot, p), sems[1].at[slot, p])

    def relay(view, sems, low, high):
        for dh in range(2):
            wait_row(view, sems, doc_row(dh, 3), low)
            send_row(view, sems, doc_row(dh, 3), low, up)
            wait_row(view, sems, doc_row(dh, 1), high)
            send_row(view, sems, doc_row(dh, 1), high, down)

    def wait_rest(view, sems, low, high):
        for dh in range(2):
            wait_row(view, sems, doc_row(dh, 3), high)
            wait_row(view, sems, doc_row(dh, 1), low)
            wait_row(view, sems, doc_row(dh, 2), low)
            wait_row(view, sems, doc_row(dh, 2), high)

    doc = (doc_view, (dp_send, dp_recv))

    for p in range(4):
        send_row(*doc, row, p, partner, up, down, src=doc_piece(p))
    remote(q_hbm, qbuf.at[x], q_send, q_recv, fsdp=device(1, 0, 0))

    w_rows = wbuf.shape[2] // PIECES
    eighth = wbuf.shape[2] // 8
    above, far, below = (z + 1) % 4, (z + 2) % 4, (z + 3) % 4

    def send_w(half, p, target):
        rows = pl.ds(p * w_rows, w_rows)
        remote(
            w_hbm.at[half, rows], wbuf.at[z, half, rows], w_send, w_recv.at[half, p], fsdp=target
        )

    def part_view(slot, p):
        owner = (far, far, below, above)[p]
        return wbuf.at[owner, (0, 1, 1, 0)[p], pl.ds(slot * eighth, eighth)]

    part = (part_view, (ws_send, ws_recv))

    for p in range(4):
        rows = pl.ds(row * eighth, eighth)
        half = (0, 1, 1, 0)[p]
        remote(
            w_hbm.at[half, rows],
            wbuf.at[z, half, rows],
            ws_send,
            ws_recv.at[row, p],
            fsdp=device(0, (2, 2, 1, 3)[p], 0),
        )

    @pl.loop(0, PIECES)
    def _(p):
        send_w(0, p, device(0, 1, 0))
        send_w(1, p, device(0, 3, 0))

    for p in (0, 1):
        wait_row(*doc, partner, p)
        send_row(*doc, partner, p, up, down)
    relay(*doc, 0, 1)
    for p in (2, 3):
        wait_row(*doc, partner, p)
        send_row(*doc, partner, p, up, down)

    def kv_view(slot, p):
        return kv.at[slot, p]

    groups = []
    for g in range(2):
        groups.append(
            Gather(
                me,
                kv_view,
                lambda p: kv.at[me, p],
                kv_send,
                kv_recv,
                (2 * g, 2 * g + 2),
                (2 * g + 2, 2 * g + 2),
            )
        )

    def choose(g):
        wait_rest(*doc, 2 * g, 2 * g + 1)
        for p in (2 * g, 2 * g + 1):
            doc_locals[p].wait()
        kv[me, pl.ds(2 * g, 2)] = (doc_a, doc_b)[g][source[row]]
        groups[g].wave1()

    def attend(g):
        groups[g].last(0, 4)

        @pl.loop(0, GROUP // 2)
        def _(k):
            for half in range(2):
                groups[g].wait(2 * k + 1 - core, 2 * g + half)

        @pl.loop(0, HEADS // 2, unroll=4)
        def _(h):
            columns = pl.ds(pl.multiple_of(h * DEPTH, DEPTH), DEPTH)
            whole = pl.ds(pl.multiple_of(h * DEPTH + g * half_width, DEPTH), DEPTH)
            keys = kv[:, 2 * g, :, columns].reshape(-1, DEPTH)
            values = kv[:, 2 * g + 1, :, columns].reshape(-1, DEPTH)
            scores = lax.dot_general(
                qbuf[:, :, whole].reshape(-1, DEPTH),
                keys,
                (((1,), (1,)), ((), ())),
                preferred_element_type=jnp.float32,
            ) * float(DEPTH) ** (-0.5)
            raised = jnp.exp(scores - jnp.max(scores, axis=1, keepdims=True))
            weights = (raised / jnp.sum(raised, axis=1, keepdims=True)).astype(jnp.bfloat16)
            mixed = jnp.dot(weights, values, preferred_element_type=jnp.float32).astype(jnp.bfloat16)
            att[core, :, :, whole] = mixed.reshape(2, tokens, DEPTH)

        done = att.at[core, :, :, pl.ds(g * half_width, half_width)]
        remote(done, done, att_send, att_recv.at[g], fsdp=device(0, 0, 1))

    choose(0)
    relay(*doc, 2, 3)
    for p in range(4):
        wait_row(*part, row, p)
        send_row(*part, row, p, partner, up, down)
    groups[0].wave2()
    groups[0].wave3()
    choose(1)
    for other in quad_peers:
        for k in range(4):
            remote(
                res_hbm.at[:, columns_of(other, k)],
                rbuf.at[quad, :, pl.ds(k * share, share)],
                r_send,
                r_recv.at[quad],
                fsdp=other,
            )

    groups[0].wave4()
    groups[0].wave5()
    groups[1].wave2()
    groups[1].wave3()
    for p in range(4):
        wait_row(*part, partner, p)
        send_row(*part, partner, p, up, down)
    locals_[0].wait()
    arrived(qbuf.at[1 - x], q_recv)
    attend(0)
    groups[1].wave4()
    groups[1].wave5()
    relay(*part, 0, 1)
    relay(*part, 2, 3)
    @pl.loop(1, GROUP)
    def _(j):
        remote(idbuf.at[me], idbuf.at[me], id_send, id_recv.at[me], fsdp=(me + j) % GROUP)


    attend(1)

    for copy in locals_[1:]:
        copy.wait()

    @pl.loop(0, PIECES)
    def _(p):
        rows = pl.ds(p * w_rows, w_rows)
        arrived(wbuf.at[below, 0, rows], w_recv.at[0, p])
        arrived(wbuf.at[above, 1, rows], w_recv.at[1, p])

    wait_rest(*part, 0, 1)
    wait_rest(*part, 2, 3)

    for other in quad_peers:
        slot = (other // 8) * 2 + other % 2
        arrived(rbuf.at[slot], r_recv.at[slot])
    for g in range(2):
        arrived(att.at[1 - core, :, :, pl.ds(g * half_width, half_width)], att_recv.at[g])

    piece = 2 * hbuf.shape[2] // HIDDEN
    quarter = hbuf.shape[3] // 4

    def hidden_view(slot, p):
        place = (slot // 8) * 2 + slot % 2
        return hbuf.at[
            (slot // 2) % 4,
            p // (HIDDEN // 2),
            pl.ds(p % (HIDDEN // 2) * piece, piece),
            pl.ds(pl.multiple_of(place * quarter, quarter), quarter),
        ]

    hg = Gather(
        me, hidden_view, lambda p: hidden_view(me, p), h_send, h_recv, (0, VIA_X), (VIA_X, HIDDEN)
    )
    def project(chip):
        def step(k, squares):
            columns = pl.ds(pl.multiple_of(k * share, share), share)
            weight = wbuf[k].reshape(-1, share)
            mixed = jnp.dot(
                att[:, chip].reshape(2 * tokens, -1), weight, preferred_element_type=jnp.float32
            )
            base = jnp.concatenate([rbuf[2 * chip + c, :, columns] for c in range(2)])
            total = mixed + base.astype(jnp.float32)
            summed[chip, :, columns] = total
            return squares + total * total

        squares = lax.fori_loop(0, 4, step, jnp.zeros((2 * tokens, share), jnp.float32))
        own = jnp.sum(squares, axis=1, keepdims=True)
        sq_out[chip] = jnp.broadcast_to(own, (2 * tokens, 128)).T[0:8]
        for other in quad_peers:
            remote(
                sq_out.at[chip], sq_in.at[chip, quad], sq_send, sq_recv.at[chip, quad], fsdp=other
            )
        sq_in[chip, quad] = sq_out[chip]

    def normalize(chip):
        for other in quad_peers:
            slot = (other // 8) * 2 + other % 2
            arrived(sq_in.at[chip, slot], sq_recv.at[chip, slot])
        mean = jnp.sum(sq_in[chip, :, 0:1], axis=0) / head_hbm.shape[1]
        scale = lax.rsqrt(mean + 1e-06)
        factor = jnp.broadcast_to(scale, (128, 2 * tokens)).T[:, 0:1]
        for k in range(4):
            columns = pl.ds(k * share, share)
            hidden = summed[chip, :, columns] * factor * gain[:, columns_of(me, k)]
            spot = pl.ds(pl.multiple_of((quad * 4 + k) * share, share), share)
            hbuf[z, chip, :, spot] = hidden.astype(jnp.bfloat16)
        hg.wave1(chip * HIDDEN // 2, (chip + 1) * HIDDEN // 2)

    project(0)
    project(1)
    normalize(0)
    normalize(1)
    arrived(head, head_sem)

    @pl.loop(1, GROUP)
    def _(j):
        other = (me + j) % GROUP
        arrived(idbuf.at[other], id_recv.at[other])

    vocab = lax.broadcasted_iota(jnp.int32, (head.shape[0], 128), 0) + me * head.shape[0]

    parts = HIDDEN // 4

    def finish(rows, slots):
        logits[...] = lax.dot_general(
            head[...], rows, (((1,), (1,)), ((), ())), preferred_element_type=jnp.float32
        )
        for c in range(2):
            slot = slots[c]
            block = logits[:, c * tokens : (c + 1) * tokens]
            largest = jnp.max(block, axis=0, keepdims=True)
            total = jnp.sum(jnp.exp(block - largest), axis=0, keepdims=True)
            picked = jnp.sum(jnp.where(vocab == idbuf[slot][0:1], block, 0.0), axis=0, keepdims=True)
            stat_out[slot, 0:1] = largest
            stat_out[slot, 1:2] = total
            stat_out[slot, 2:3] = picked
            stat_out[slot, 3:8] = jnp.zeros((5, tokens), jnp.float32)

            @pl.when(slot != me)
            def _():
                remote(stat_out.at[slot], stat_in.at[me], stat_send, stat_recv.at[me], fsdp=slot)

    def wait_other_core(spot, low, high):
        for dx in range(2):
            slot = dx * 8 + spot * 2 + 1 - core
            pl.loop(low, high)(lambda p: hg.wait(slot, p))

    @pl.loop(0, 6)
    def _(step):
        for when, wave in ((0, hg.wave2), (1, hg.wave3), (2, hg.wave4), (4, hg.wave5)):
            pl.when(step == when)(wave)
        chip = jnp.where(step < 2, step, (step - 2) // 2)
        dz = jnp.where(step < 2, 0, 1 + 2 * (step % 2))
        spot = (z + dz) % 4
        wait_other_core(spot, chip * 2 * parts, chip * 2 * parts + 2 * parts)
        slot = chip * 8 + spot * 2
        finish(hbuf[spot, chip], (slot, slot + 1))

    spot = (z + 2) % 4

    @pl.loop(0, 2)
    def _(c):
        for k in range(2):

            @pl.when(c == k)
            def _():
                hg.last(k * parts, k * parts + parts)
                hg.last((2 + k) * parts, (3 + k) * parts)

        wait_other_core(spot, c * parts, c * parts + parts)
        wait_other_core(spot, (2 + c) * parts, (2 + c) * parts + parts)
        rows = hbuf[spot, :, pl.ds(pl.multiple_of(c * tokens, tokens), tokens)]
        finish(rows.reshape(2 * tokens, -1), (spot * 2 + c, 8 + spot * 2 + c))

    stat_in[me] = stat_out[me]

    @pl.loop(1, GROUP)
    def _(j):
        other = (me + j) % GROUP
        arrived(stat_in.at[other], stat_recv.at[other])

    largest = stat_in[:, 0, :]
    highest = jnp.max(largest, axis=0, keepdims=True)
    total = jnp.sum(stat_in[:, 1, :] * jnp.exp(largest - highest), axis=0, keepdims=True)
    picked = jnp.sum(stat_in[:, 2, :], axis=0, keepdims=True)
    new = picked - (highest + jnp.log(total))
    position = core * tokens + lax.broadcasted_iota(jnp.int32, (1, 128), 1)
    live = position < lengths[0, me // 2]
    before = old[...]
    out[0:1] = jnp.where(live, new - before, 0.0)
    gap = jnp.clip(before - new, -3.0, 3.0)
    out[1:2] = jnp.where(live, jnp.exp(gap) - gap - 1.0, 0.0)

    arrived(sq_in.at[:, pl.ds(0, 3)], sq_send)
    arrived(hbuf.at[:, :, pl.ds(0, 15 * hbuf.shape[2] // 16)], h_send)
    for buf, count, sem in (
        (kv, 15, kv_send),
        (wbuf, 1, w_send),
        (wbuf, 2, ws_send),
        (kv, 7, dp_send),
        (rbuf, 3, r_send),
        (qbuf, 1, q_send),
        (att, 1, att_send),
        (idbuf, 15, id_send),
        (stat_out, 15, stat_send),
    ):
        view = buf.at[pl.ds(0, count)]
        arrived(view, sem)


def on_device(
    queries, doc_kv, residual, out_weight, out_gain, head, source, lengths, sampled, old_logprob
):
    tokens, width = queries.shape
    columns = residual.shape[1]
    share = out_weight.shape[1]
    positions = doc_kv.shape[2]
    bf16, f32 = jnp.bfloat16, jnp.float32
    smem = pl.BlockSpec(memory_space=pltpu.SMEM)
    vmem = pl.BlockSpec(memory_space=pltpu.VMEM)
    any_ = pl.BlockSpec(memory_space=pl.ANY)
    dma = pltpu.SemaphoreType.DMA
    both = pl.pallas_call(
        kernel,
        out_shape=jax.ShapeDtypeStruct((2, tokens), f32),
        in_specs=[smem, smem, vmem, vmem, vmem] + [any_] * 5,
        out_specs=vmem,
        scratch_shapes=[
            pltpu.VMEM(head.shape, bf16),
            pltpu.VMEM((4, 2, width // 2, share), bf16),
            pltpu.VMEM((4, 2, 2 * tokens, columns), bf16),
            pltpu.VMEM((ROWS, 2, positions, width // 2), bf16),
            pltpu.VMEM((ROWS, 2, positions, width // 2), bf16),
            pltpu.VMEM((GROUP, 4, positions, width // 2), bf16),
            pltpu.VMEM((2, tokens, width), bf16),
            pltpu.VMEM((4, tokens, columns // 4), bf16),
            pltpu.VMEM((2, 2, tokens, width), bf16),
            pltpu.VMEM((2, 2 * tokens, columns // 4), f32),
            pltpu.VMEM((head.shape[0], 256), f32),
            pltpu.VMEM((GROUP, 8, 128), jnp.int32),
            pltpu.VMEM((2, 8, 2 * tokens), f32),
            pltpu.VMEM((2, 4, 8, 2 * tokens), f32),
            pltpu.VMEM((GROUP, 8, 128), f32),
            pltpu.VMEM((GROUP, 8, 128), f32),
            dma((10,)),
            dma,
            dma,
            dma((2, PIECES)),
            dma,
            dma((ROWS, 4)),
            dma,
            dma((GROUP, HIDDEN)),
            dma,
            dma((GROUP, 4)),
            dma,
            dma((ROWS, 4)),
            dma,
            dma,
            dma,
            dma((4,)),
            dma,
            dma((2,)),
            dma,
            dma((2, 4)),
            dma,
            dma((GROUP,)),
            dma,
            dma((GROUP,)),
        ],
        compiler_params=pltpu.CompilerParams(
            collective_id=0, has_side_effects=True, vmem_limit_bytes=60 * 1024 * 1024
        ),
    )(
        source,
        lengths,
        sampled.reshape(1, tokens),
        old_logprob.reshape(1, tokens),
        out_gain.reshape(1, columns),
        queries,
        doc_kv.reshape(2, positions, width),
        residual,
        out_weight.reshape(2, width // 2, share),
        head,
    )
    return both[0], both[1]


def solution(mesh):
    return jax.shard_map(
        on_device,
        mesh=mesh,
        in_specs=(
            P(("dp", "fsdp"), None),
            P(None, "dp", "fsdp", None),
            P(("dp", "fsdp"), None),
            P(None, "fsdp"),
            P(),
            P("fsdp", None),
            P(),
            P("dp", None),
            P(("dp", "fsdp")),
            P(("dp", "fsdp")),
        ),
        out_specs=(P(("dp", "fsdp")), P(("dp", "fsdp"))),
        check_vma=False,
    )
```

```python
import jax
import jax.numpy as jnp
from jax import lax
from jax.experimental import pallas as pl
from jax.experimental.pallas import tpu as pltpu
from jax.sharding import PartitionSpec as P

HEADS = 8
DEPTH = 256
GROUP = 16
ROWS = 8
MESH = pl.DeviceIdType.MESH
PIECES = 4
HIDDEN = 16
VIA_X = 9


class Gather:
    def __init__(self, me, view, own, send_sem, recv_sem, first, second):
        self.me, self.view, self.own = me, view, own
        self.send_sem, self.recv_sem = send_sem, recv_sem
        self.first, self.second = first, second
        self.middle = (second[0] + second[1] + 1) // 2
        x, z, core = me // 8, (me // 2) % 4, me % 2

        def slot(dx, dz):
            return ((x + dx) % 2) * 8 + ((z + dz) % 4) * 2 + core

        self.x, self.zp, self.zm, self.z2 = slot(1, 0), slot(0, 1), slot(0, 3), slot(0, 2)
        self.xzp, self.xzm, self.xz2 = slot(1, 1), slot(1, 3), slot(1, 2)
        self.core = me + 1 - 2 * core

    def send(self, slot, p, *targets, own=False):
        dst = self.view(slot, p)
        src = self.own(p) if own else dst
        for target in targets:
            pltpu.make_async_remote_copy(
                src_ref=src,
                dst_ref=dst,
                send_sem=self.send_sem,
                recv_sem=self.recv_sem.at[slot, p],
                device_id={"fsdp": target},
                device_id_type=MESH,
            ).start()

    def wait(self, slot, p):
        view = self.view(slot, p)
        pltpu.make_async_copy(view, view, self.recv_sem.at[slot, p]).wait()

    def pass_on(self, slot, p, *targets):
        self.wait(slot, p)
        self.send(slot, p, *targets, self.core)

    def each(self, low, high, step):
        if high - low == 1:
            step(low)
        elif high > low:
            pl.loop(low, high)(step)

    def wave1(self, low=0, high=1 << 10):
        first = max(low, self.first[0]), min(high, self.first[1])
        second = max(low, self.second[0]), min(high, self.second[1])
        self.each(*first, lambda p: self.send(self.me, p, self.x, own=True))
        self.each(*second, lambda p: self.send(self.me, p, self.zp, self.zm, own=True))
        self.each(*first, lambda p: self.send(self.me, p, self.zp, self.zm, self.core, own=True))
        self.each(*second, lambda p: self.send(self.me, p, self.x, self.core, own=True))

    def wave2(self):
        self.each(*self.first, lambda p: self.pass_on(self.x, p, self.zp, self.zm))

    def wave3(self):
        def up(p):
            self.pass_on(self.zp, p, self.x)
            self.pass_on(self.zm, p, self.zp, self.x)

        def down(p):
            self.pass_on(self.zp, p, self.zm, self.x)
            self.pass_on(self.zm, p, self.x)

        def own_side(p):
            self.pass_on(self.zm, p, self.zp)
            self.pass_on(self.zp, p)

        self.each(self.second[0], self.middle, down)
        self.each(self.middle, self.second[1], up)
        self.each(*self.first, own_side)
        self.each(*self.second, lambda p: self.pass_on(self.x, p))

    def wave4(self):
        def far_side(p):
            self.pass_on(self.xzp, p, self.zm)
            self.pass_on(self.xzm, p)

        self.each(*self.first, far_side)

    def wave5(self):
        def far_side(p):
            self.pass_on(self.xzp, p)
            self.pass_on(self.xzm, p)

        self.each(*self.second, lambda p: self.pass_on(self.z2, p, self.x))
        self.each(*self.second, far_side)

    def last(self, low, high):
        def step(p):
            self.pass_on(self.z2, p)
            self.pass_on(self.xz2, p)

        self.each(max(low, self.first[0]), min(high, self.first[1]), step)
        self.each(
            max(low, self.second[0]), min(high, self.second[1]), lambda p: self.pass_on(self.xz2, p)
        )


def kernel(
    source,
    lengths,
    ids,
    old,
    gain,
    q_hbm,
    doc_hbm,
    res_hbm,
    w_hbm,
    head_hbm,
    out,
    head,
    wbuf,
    hbuf,
    doc_a,
    doc_b,
    kv,
    qbuf,
    rbuf,
    att,
    summed,
    logits,
    idbuf,
    sq_out,
    sq_in,
    stat_out,
    stat_in,
    local_sems,
    head_sem,
    w_send,
    w_recv,
    ws_send,
    ws_recv,
    h_send,
    h_recv,
    kv_send,
    kv_recv,
    dp_send,
    dp_recv,
    q_send,
    q_recv,
    r_send,
    r_recv,
    att_send,
    att_recv,
    sq_send,
    sq_recv,
    id_send,
    id_recv,
    stat_send,
    stat_recv,
):
    row = lax.axis_index("dp")
    me = lax.axis_index("fsdp")
    x, z, core = me // 8, (me // 2) % 4, me % 2
    xh, y = row // 4, row % 4
    quad = x * 2 + core
    share = wbuf.shape[3]
    tokens = qbuf.shape[1]

    def device(dx, dz, dc):
        return ((x + dx) % 2) * 8 + ((z + dz) % 4) * 2 + (core + dc) % 2

    def doc_row(dh, dy):
        return ((xh + dh) % 2) * 4 + (y + dy) % 4

    def columns_of(other, k):
        block = (other // 8) * 8 + k * 2 + other % 2
        return pl.ds(pl.multiple_of(block * share, share), share)

    def remote(src, dst, send, recv, **where):
        pltpu.make_async_remote_copy(
            src_ref=src, dst_ref=dst, send_sem=send, recv_sem=recv, device_id=where, device_id_type=MESH
        ).start()

    def arrived(view, sem):
        pltpu.make_async_copy(view, view, sem).wait()

    barrier = pltpu.get_barrier_semaphore()

    @pl.loop(1, GROUP)
    def _(j):
        pl.semaphore_signal(barrier, inc=1, device_id={"fsdp": (me + j) % GROUP}, device_id_type=MESH)

    near_rows = (doc_row(1, 0), doc_row(0, 1), doc_row(0, 3))
    for other in near_rows:
        pl.semaphore_signal(barrier, inc=1, device_id={"dp": other}, device_id_type=MESH)

    half_width = kv.shape[3]

    def doc_piece(p):
        return doc_hbm.at[p % 2, :, pl.ds(p // 2 * half_width, half_width)]

    def doc_view(slot, p):
        return (doc_a, doc_b)[p // 2].at[slot, p % 2]

    locals_ = [
        pltpu.make_async_copy(q_hbm, qbuf.at[x], local_sems.at[0]),
        pltpu.make_async_copy(w_hbm, wbuf.at[z], local_sems.at[1]),
    ] + [
        pltpu.make_async_copy(
            res_hbm.at[:, columns_of(me, k)],
            rbuf.at[quad, :, pl.ds(k * share, share)],
            local_sems.at[2 + k],
        )
        for k in range(4)
    ]
    doc_locals = [
        pltpu.make_async_copy(doc_piece(p), doc_view(row, p), local_sems.at[6 + p]) for p in range(4)
    ]
    for copy in doc_locals + locals_:
        copy.start()
    idbuf[me] = jnp.broadcast_to(ids[...], (8, 128))

    pl.semaphore_wait(barrier, GROUP - 1 + 3)

    quad_peers = (device(1, 0, 0), device(0, 0, 1), device(1, 0, 1))
    partner, up, down = near_rows

    def send_row(view, sems, slot, p, *targets, src=None):
        dst = view(slot, p)
        for target in targets:
            remote(dst if src is None else src, dst, sems[0], sems[1].at[slot, p], dp=target)

    def wait_row(view, sems, slot, p):
        arrived(view(slot, p), sems[1].at[slot, p])

    def relay(view, sems, low, high):
        for dh in range(2):
            wait_row(view, sems, doc_row(dh, 3), low)
            send_row(view, sems, doc_row(dh, 3), low, up)
            wait_row(view, sems, doc_row(dh, 1), high)
            send_row(view, sems, doc_row(dh, 1), high, down)

    def wait_rest(view, sems, low, high):
        for dh in range(2):
            wait_row(view, sems, doc_row(dh, 3), high)
            wait_row(view, sems, doc_row(dh, 1), low)
            wait_row(view, sems, doc_row(dh, 2), low)
            wait_row(view, sems, doc_row(dh, 2), high)

    doc = (doc_view, (dp_send, dp_recv))

    for p in range(4):
        send_row(*doc, row, p, partner, up, down, src=doc_piece(p))
    remote(q_hbm, qbuf.at[x], q_send, q_recv, fsdp=device(1, 0, 0))

    w_rows = wbuf.shape[2] // PIECES
    eighth = wbuf.shape[2] // 8
    above, far, below = (z + 1) % 4, (z + 2) % 4, (z + 3) % 4

    def send_w(half, p, target):
        rows = pl.ds(p * w_rows, w_rows)
        remote(
            w_hbm.at[half, rows], wbuf.at[z, half, rows], w_send, w_recv.at[half, p], fsdp=target
        )

    def part_view(slot, p):
        owner = (far, far, below, above)[p]
        return wbuf.at[owner, (0, 1, 1, 0)[p], pl.ds(slot * eighth, eighth)]

    part = (part_view, (ws_send, ws_recv))

    for p in range(4):
        rows = pl.ds(row * eighth, eighth)
        half = (0, 1, 1, 0)[p]
        remote(
            w_hbm.at[half, rows],
            wbuf.at[z, half, rows],
            ws_send,
            ws_recv.at[row, p],
            fsdp=device(0, (2, 2, 1, 3)[p], 0),
        )

    @pl.loop(0, PIECES)
    def _(p):
        send_w(0, p, device(0, 1, 0))
        send_w(1, p, device(0, 3, 0))

    for k in range(GROUP):
        pltpu.make_async_copy(
            head_hbm.at[:, pl.ds(k * share, share)],
            head.at[:, pl.ds(((k // 8 * 2 + k % 2) * 4 + k // 2 % 4) * share, share)],
            head_sem,
        ).start()

    for p in (0, 1):
        wait_row(*doc, partner, p)
        send_row(*doc, partner, p, up, down)
    relay(*doc, 0, 1)
    for p in (2, 3):
        wait_row(*doc, partner, p)
        send_row(*doc, partner, p, up, down)

    def kv_view(slot, p):
        return kv.at[slot, p]

    groups = []
    for g in range(2):
        groups.append(
            Gather(
                me,
                kv_view,
                lambda p: kv.at[me, p],
                kv_send,
                kv_recv,
                (2 * g, 2 * g + 2),
                (2 * g + 2, 2 * g + 2),
            )
        )

    def choose(g):
        wait_rest(*doc, 2 * g, 2 * g + 1)
        for p in (2 * g, 2 * g + 1):
            doc_locals[p].wait()
        kv[me, pl.ds(2 * g, 2)] = (doc_a, doc_b)[g][source[row]]
        groups[g].wave1()

    def attend(g):
        groups[g].last(0, 4)

        @pl.loop(0, GROUP // 2)
        def _(k):
            for half in range(2):
                groups[g].wait(2 * k + 1 - core, 2 * g + half)

        @pl.loop(0, HEADS // 2, unroll=4)
        def _(h):
            columns = pl.ds(pl.multiple_of(h * DEPTH, DEPTH), DEPTH)
            whole = pl.ds(pl.multiple_of(h * DEPTH + g * half_width, DEPTH), DEPTH)
            keys = kv[:, 2 * g, :, columns].reshape(-1, DEPTH)
            values = kv[:, 2 * g + 1, :, columns].reshape(-1, DEPTH)
            scores = lax.dot_general(
                qbuf[:, :, whole].reshape(-1, DEPTH),
                keys,
                (((1,), (1,)), ((), ())),
                preferred_element_type=jnp.float32,
            ) * float(DEPTH) ** (-0.5)
            raised = jnp.exp(scores - jnp.max(scores, axis=1, keepdims=True))
            weights = (raised / jnp.sum(raised, axis=1, keepdims=True)).astype(jnp.bfloat16)
            mixed = jnp.dot(weights, values, preferred_element_type=jnp.float32).astype(jnp.bfloat16)
            att[core, :, :, whole] = mixed.reshape(2, tokens, DEPTH)

        done = att.at[core, :, :, pl.ds(g * half_width, half_width)]
        remote(done, done, att_send, att_recv.at[g], fsdp=device(0, 0, 1))

    choose(0)
    relay(*doc, 2, 3)
    for p in range(4):
        wait_row(*part, row, p)
        send_row(*part, row, p, partner, up, down)
    groups[0].wave2()
    groups[0].wave3()
    choose(1)
    for other in quad_peers:
        for k in range(4):
            remote(
                res_hbm.at[:, columns_of(other, k)],
                rbuf.at[quad, :, pl.ds(k * share, share)],
                r_send,
                r_recv.at[quad],
                fsdp=other,
            )

    groups[0].wave4()
    groups[0].wave5()
    groups[1].wave2()
    groups[1].wave3()
    for p in range(4):
        wait_row(*part, partner, p)
        send_row(*part, partner, p, up, down)
    locals_[0].wait()
    arrived(qbuf.at[1 - x], q_recv)
    attend(0)
    groups[1].wave4()
    groups[1].wave5()
    relay(*part, 0, 1)
    relay(*part, 2, 3)
    attend(1)

    for copy in locals_[1:]:
        copy.wait()

    @pl.loop(0, PIECES)
    def _(p):
        rows = pl.ds(p * w_rows, w_rows)
        arrived(wbuf.at[below, 0, rows], w_recv.at[0, p])
        arrived(wbuf.at[above, 1, rows], w_recv.at[1, p])

    wait_rest(*part, 0, 1)
    wait_rest(*part, 2, 3)

    for other in quad_peers:
        slot = (other // 8) * 2 + other % 2
        arrived(rbuf.at[slot], r_recv.at[slot])
    for g in range(2):
        arrived(att.at[1 - core, :, :, pl.ds(g * half_width, half_width)], att_recv.at[g])

    piece = 2 * hbuf.shape[2] // HIDDEN
    quarter = hbuf.shape[3] // 4

    def hidden_view(slot, p):
        place = (slot // 8) * 2 + slot % 2
        return hbuf.at[
            (slot // 2) % 4,
            p // (HIDDEN // 2),
            pl.ds(p % (HIDDEN // 2) * piece, piece),
            pl.ds(pl.multiple_of(place * quarter, quarter), quarter),
        ]

    hg = Gather(
        me, hidden_view, lambda p: hidden_view(me, p), h_send, h_recv, (0, VIA_X), (VIA_X, HIDDEN)
    )
    def project(chip):
        def step(k, squares):
            columns = pl.ds(pl.multiple_of(k * share, share), share)
            weight = wbuf[k].reshape(-1, share)
            mixed = jnp.dot(
                att[:, chip].reshape(2 * tokens, -1), weight, preferred_element_type=jnp.float32
            )
            base = jnp.concatenate([rbuf[2 * chip + c, :, columns] for c in range(2)])
            total = mixed + base.astype(jnp.float32)
            summed[chip, :, columns] = total
            return squares + total * total

        squares = lax.fori_loop(0, 4, step, jnp.zeros((2 * tokens, share), jnp.float32), unroll=True)
        own = jnp.sum(squares, axis=1, keepdims=True)
        sq_out[chip] = jnp.broadcast_to(own, (2 * tokens, 128)).T[0:8]
        for other in quad_peers:
            remote(
                sq_out.at[chip], sq_in.at[chip, quad], sq_send, sq_recv.at[chip, quad], fsdp=other
            )
        sq_in[chip, quad] = sq_out[chip]

    def normalize(chip):
        for other in quad_peers:
            slot = (other // 8) * 2 + other % 2
            arrived(sq_in.at[chip, slot], sq_recv.at[chip, slot])
        mean = jnp.sum(sq_in[chip, :, 0:1], axis=0) / head_hbm.shape[1]
        scale = lax.rsqrt(mean + 1e-06)
        factor = jnp.broadcast_to(scale, (128, 2 * tokens)).T[:, 0:1]
        for k in range(4):
            columns = pl.ds(k * share, share)
            hidden = summed[chip, :, columns] * factor * gain[:, columns_of(me, k)]
            spot = pl.ds(pl.multiple_of((quad * 4 + k) * share, share), share)
            hbuf[z, chip, :, spot] = hidden.astype(jnp.bfloat16)
        hg.wave1(chip * HIDDEN // 2, (chip + 1) * HIDDEN // 2)

    project(0)
    project(1)

    @pl.loop(1, GROUP)
    def _(j):
        remote(idbuf.at[me], idbuf.at[me], id_send, id_recv.at[me], fsdp=(me + j) % GROUP)

    normalize(0)
    normalize(1)
    arrived(head, head_sem)

    @pl.loop(1, GROUP)
    def _(j):
        other = (me + j) % GROUP
        arrived(idbuf.at[other], id_recv.at[other])

    vocab = lax.broadcasted_iota(jnp.int32, (head.shape[0], 128), 0) + me * head.shape[0]

    parts = HIDDEN // 4

    def finish(rows, slots):
        logits[...] = lax.dot_general(
            head[...], rows, (((1,), (1,)), ((), ())), preferred_element_type=jnp.float32
        )
        for c in range(2):
            slot = slots[c]
            block = logits[:, c * tokens : (c + 1) * tokens]
            largest = jnp.max(block, axis=0, keepdims=True)
            total = jnp.sum(jnp.exp(block - largest), axis=0, keepdims=True)
            picked = jnp.sum(jnp.where(vocab == idbuf[slot][0:1], block, 0.0), axis=0, keepdims=True)
            stat_out[slot, 0:1] = largest
            stat_out[slot, 1:2] = total
            stat_out[slot, 2:3] = picked
            stat_out[slot, 3:8] = jnp.zeros((5, tokens), jnp.float32)

            @pl.when(slot != me)
            def _():
                remote(stat_out.at[slot], stat_in.at[me], stat_send, stat_recv.at[me], fsdp=slot)

    def wait_other_core(spot, low, high):
        for dx in range(2):
            slot = dx * 8 + spot * 2 + 1 - core
            pl.loop(low, high)(lambda p: hg.wait(slot, p))

    @pl.loop(0, 6)
    def _(step):
        for when, wave in ((0, hg.wave2), (1, hg.wave3), (2, hg.wave4), (4, hg.wave5)):
            pl.when(step == when)(wave)
        chip = jnp.where(step < 2, step, (step - 2) // 2)
        dz = jnp.where(step < 2, 0, 1 + 2 * (step % 2))
        spot = (z + dz) % 4
        wait_other_core(spot, chip * 2 * parts, chip * 2 * parts + 2 * parts)
        slot = chip * 8 + spot * 2
        finish(hbuf[spot, chip], (slot, slot + 1))

    spot = (z + 2) % 4

    @pl.loop(0, 2)
    def _(c):
        for k in range(2):

            @pl.when(c == k)
            def _():
                hg.last(k * parts, k * parts + parts)
                hg.last((2 + k) * parts, (3 + k) * parts)

        wait_other_core(spot, c * parts, c * parts + parts)
        wait_other_core(spot, (2 + c) * parts, (2 + c) * parts + parts)
        rows = hbuf[spot, :, pl.ds(pl.multiple_of(c * tokens, tokens), tokens)]
        finish(rows.reshape(2 * tokens, -1), (spot * 2 + c, 8 + spot * 2 + c))

    stat_in[me] = stat_out[me]

    @pl.loop(1, GROUP)
    def _(j):
        other = (me + j) % GROUP
        arrived(stat_in.at[other], stat_recv.at[other])

    largest = stat_in[:, 0, :]
    highest = jnp.max(largest, axis=0, keepdims=True)
    total = jnp.sum(stat_in[:, 1, :] * jnp.exp(largest - highest), axis=0, keepdims=True)
    picked = jnp.sum(stat_in[:, 2, :], axis=0, keepdims=True)
    new = picked - (highest + jnp.log(total))
    position = core * tokens + lax.broadcasted_iota(jnp.int32, (1, 128), 1)
    live = position < lengths[0, me // 2]
    before = old[...]
    out[0:1] = jnp.where(live, new - before, 0.0)
    gap = jnp.clip(before - new, -3.0, 3.0)
    out[1:2] = jnp.where(live, jnp.exp(gap) - gap - 1.0, 0.0)

    arrived(sq_in.at[:, pl.ds(0, 3)], sq_send)
    arrived(hbuf.at[:, :, pl.ds(0, 15 * hbuf.shape[2] // 16)], h_send)
    for buf, count, sem in (
        (kv, 15, kv_send),
        (wbuf, 1, w_send),
        (wbuf, 2, ws_send),
        (kv, 7, dp_send),
        (rbuf, 3, r_send),
        (qbuf, 1, q_send),
        (att, 1, att_send),
        (idbuf, 15, id_send),
        (stat_out, 15, stat_send),
    ):
        view = buf.at[pl.ds(0, count)]
        arrived(view, sem)


def on_device(
    queries, doc_kv, residual, out_weight, out_gain, head, source, lengths, sampled, old_logprob
):
    tokens, width = queries.shape
    columns = residual.shape[1]
    share = out_weight.shape[1]
    positions = doc_kv.shape[2]
    bf16, f32 = jnp.bfloat16, jnp.float32
    smem = pl.BlockSpec(memory_space=pltpu.SMEM)
    vmem = pl.BlockSpec(memory_space=pltpu.VMEM)
    any_ = pl.BlockSpec(memory_space=pl.ANY)
    dma = pltpu.SemaphoreType.DMA
    both = pl.pallas_call(
        kernel,
        out_shape=jax.ShapeDtypeStruct((2, tokens), f32),
        in_specs=[smem, smem, vmem, vmem, vmem] + [any_] * 5,
        out_specs=vmem,
        scratch_shapes=[
            pltpu.VMEM(head.shape, bf16),
            pltpu.VMEM((4, 2, width // 2, share), bf16),
            pltpu.VMEM((4, 2, 2 * tokens, columns), bf16),
            pltpu.VMEM((ROWS, 2, positions, width // 2), bf16),
            pltpu.VMEM((ROWS, 2, positions, width // 2), bf16),
            pltpu.VMEM((GROUP, 4, positions, width // 2), bf16),
            pltpu.VMEM((2, tokens, width), bf16),
            pltpu.VMEM((4, tokens, columns // 4), bf16),
            pltpu.VMEM((2, 2, tokens, width), bf16),
            pltpu.VMEM((2, 2 * tokens, columns // 4), f32),
            pltpu.VMEM((head.shape[0], 256), f32),
            pltpu.VMEM((GROUP, 8, 128), jnp.int32),
            pltpu.VMEM((2, 8, 2 * tokens), f32),
            pltpu.VMEM((2, 4, 8, 2 * tokens), f32),
            pltpu.VMEM((GROUP, 8, 128), f32),
            pltpu.VMEM((GROUP, 8, 128), f32),
            dma((10,)),
            dma,
            dma,
            dma((2, PIECES)),
            dma,
            dma((ROWS, 4)),
            dma,
            dma((GROUP, HIDDEN)),
            dma,
            dma((GROUP, 4)),
            dma,
            dma((ROWS, 4)),
            dma,
            dma,
            dma,
            dma((4,)),
            dma,
            dma((2,)),
            dma,
            dma((2, 4)),
            dma,
            dma((GROUP,)),
            dma,
            dma((GROUP,)),
        ],
        compiler_params=pltpu.CompilerParams(
            collective_id=0, has_side_effects=True, vmem_limit_bytes=60 * 1024 * 1024
        ),
    )(
        source,
        lengths,
        sampled.reshape(1, tokens),
        old_logprob.reshape(1, tokens),
        out_gain.reshape(1, columns),
        queries,
        doc_kv.reshape(2, positions, width),
        residual,
        out_weight.reshape(2, width // 2, share),
        head,
    )
    return both[0], both[1]


def solution(mesh):
    return jax.shard_map(
        on_device,
        mesh=mesh,
        in_specs=(
            P(("dp", "fsdp"), None),
            P(None, "dp", "fsdp", None),
            P(("dp", "fsdp"), None),
            P(None, "fsdp"),
            P(),
            P("fsdp", None),
            P(),
            P("dp", None),
            P(("dp", "fsdp")),
            P(("dp", "fsdp")),
        ),
        out_specs=(P(("dp", "fsdp")), P(("dp", "fsdp"))),
        check_vma=False,
    )
```
